256 devices in a mesh: inp: 8 (over z_lo, x), out: 4 (over y), dep: 8 (over z_hi, core).
Axes of the slice: x: 4, y: 4, z: 8 (z_hi: 4, z_lo: 2; z = z_hi * 2 + z_lo), core: 2. Of those that a mesh axis runs over, the one named last changes fastest.
Arguments:
- tokens: bfloat16 [1024, 4096], P(('dep', 'out'), 'inp'), may hold values from -6 to 6
- cotangent: bfloat16 [1024, 4096], P(('dep', 'out'), 'inp'), may hold values from -3 to 3
- gate_weight: bfloat16 [4096, 14336], P(('inp', 'dep'), 'out'), may hold values from -0.09375 to 0.09375
- up_weight: bfloat16 [4096, 14336], P(('inp', 'dep'), 'out'), may hold values from -0.09375 to 0.09375
- down_weight: bfloat16 [14336, 4096], P(('out', 'dep'), 'inp'), may hold values from -0.046875 to 0.046875
Outputs:
- token_grad: float32 [1024, 4096], P(('dep', 'out'), 'inp')
- gate_weight_grad: float32 [4096, 14336], P(('inp', 'dep'), 'out')
- up_weight_grad: float32 [4096, 14336], P(('inp', 'dep'), 'out')
- down_weight_grad: float32 [14336, 4096], P(('out', 'dep'), 'inp')
The draws below stay inside these ranges and needn't reach their ends.
All inputs are finite; a program needn't handle non-finite values.
Results may differ from the reference program's by a relative error of at most 0.019.
Values may be sent and summed in bfloat16 or wider, within the bound.
A program may use at most 128 MiB of HBM per device.

```python
import jax
import jax.numpy as jnp
from jax import lax

D = 4096
FF = 14336
TOK_DEV = 128
TOKENS = 1024


def steps_of(rng, dims, cuts, smallest, largest):
    def one(axis_at, parts):
        steps = jax.random.uniform(jax.random.fold_in(jax.random.fold_in(rng, 6), axis_at), (parts,), jnp.float32, smallest / len(cuts), largest / len(cuts))
        return jnp.repeat(jnp.exp(steps), dims[axis_at] // parts).reshape((-1,) + (1,) * (len(dims) - axis_at - 1))

    factor_of = one(*cuts[0])
    for cut in cuts[1:]:
        factor_of = factor_of * one(*cut)
    return factor_of


def gaussian(rng, shape, deviation, limit, cuts=(), kind=jnp.bfloat16):
    factor_of = steps_of(rng, shape, cuts, -0.22, 0.18) if cuts else 1.0
    entries = jax.random.normal(rng, shape, jnp.float32) * deviation * factor_of
    return jnp.minimum(jnp.maximum(entries, -limit), limit).astype(kind)


def setup_inputs(seed: int = 0) -> dict:
    seeds = jax.random.split(jax.random.key(seed), 6)
    tokens = gaussian(seeds[0], (TOKENS, D), 1.0, 6.0, ((0, 32), (1, 8)))
    cotangent = gaussian(seeds[1], (TOKENS, D), 0.5, 3.0, ((0, 32), (1, 8)))
    gate_weight = gaussian(seeds[2], (D, FF), D ** -0.5, 0.09375, ((0, 64), (1, 4)))
    up_weight = gaussian(seeds[3], (D, FF), D ** -0.5, 0.09375, ((0, 64), (1, 4)))
    down_weight = gaussian(seeds[4], (FF, D), FF ** -0.5, 0.046875, ((0, 32), (1, 8)))
    return {"tokens": tokens, "cotangent": cotangent, "gate_weight": gate_weight, "up_weight": up_weight, "down_weight": down_weight}


def contract_last(left_side, right_side):
    return lax.dot_general(left_side, right_side, (((1,), (1,)), ((), ())), preferred_element_type=jnp.float32)


def contract_first(left_side, right_side):
    return lax.dot_general(left_side, right_side, (((0,), (0,)), ((), ())), preferred_element_type=jnp.float32)


def rounded(value):
    return lax.optimization_barrier(value.astype(jnp.bfloat16)).astype(jnp.float32)


def reference(tokens, cotangent, gate_weight, up_weight, down_weight):
    gate_value = jnp.dot(tokens, gate_weight, preferred_element_type=jnp.float32)
    up_value = jnp.dot(tokens, up_weight, preferred_element_type=jnp.float32)
    hidden_grad = contract_last(cotangent, down_weight)
    logistic = jax.nn.sigmoid(gate_value)
    activated = gate_value * logistic
    hidden = (activated * up_value).astype(jnp.bfloat16)
    up_grad = (hidden_grad * activated).astype(jnp.bfloat16)
    gate_grad = (hidden_grad * up_value * logistic * (1.0 + gate_value * (1.0 - logistic))).astype(jnp.bfloat16)
    token_grad = contract_last(gate_grad, gate_weight) + contract_last(up_grad, up_weight)

    def accumulate(running, block_index):
        first_row = (block_index * TOK_DEV).astype(jnp.int32)
        block_tokens = lax.dynamic_slice_in_dim(tokens, first_row, TOK_DEV, 0)
        block_cotangent = lax.dynamic_slice_in_dim(cotangent, first_row, TOK_DEV, 0)
        block_hidden = lax.dynamic_slice_in_dim(hidden, first_row, TOK_DEV, 0)
        block_gate = lax.dynamic_slice_in_dim(gate_grad, first_row, TOK_DEV, 0)
        block_up = lax.dynamic_slice_in_dim(up_grad, first_row, TOK_DEV, 0)
        gate_total = running[0] + rounded(contract_first(block_tokens, block_gate))
        up_total = running[1] + rounded(contract_first(block_tokens, block_up))
        down_total = running[2] + rounded(contract_first(block_hidden, block_cotangent))
        return (gate_total, up_total, down_total), None

    initial = (jnp.zeros((D, FF), jnp.float32), jnp.zeros((D, FF), jnp.float32), jnp.zeros((FF, D), jnp.float32))
    totals, unused = lax.scan(accumulate, initial, jnp.arange(TOKENS // TOK_DEV, dtype=jnp.int32))
    return (token_grad, totals[0], totals[1], totals[2])
```

```python
import jax
import jax.numpy as jnp
from jax import lax
from jax.sharding import PartitionSpec as P


def contract_last(left_side, right_side):
    return lax.dot_general(
        left_side, right_side, (((1,), (1,)), ((), ())), preferred_element_type=jnp.float32
    )


def contract_first(left_side, right_side):
    return lax.dot_general(
        left_side, right_side, (((0,), (0,)), ((), ())), preferred_element_type=jnp.float32
    )


def local_step(gate_value, up_value, hidden_grad):
    logistic = jax.nn.sigmoid(gate_value)
    activated = gate_value * logistic
    hidden = (activated * up_value).astype(jnp.bfloat16)
    up_grad = (hidden_grad * activated).astype(jnp.bfloat16)
    gate_grad = (hidden_grad * up_value * logistic * (1.0 + gate_value * (1.0 - logistic))).astype(
        jnp.bfloat16
    )
    return (hidden, gate_grad, up_grad)


def shards(tokens, cotangent, gate_weight, up_weight, down_weight):
    n_inp = lax.axis_size("inp")
    both = jnp.concatenate((tokens, cotangent), axis=1)
    both = lax.all_gather(both, ("dep", "out"), axis=0, tiled=True)
    width = tokens.shape[1]
    all_tokens, all_cotangent = both[:, :width], both[:, width:]
    weights = jnp.stack((gate_weight, up_weight))
    weights = lax.all_to_all(weights, "dep", split_axis=2, concat_axis=1, tiled=True)
    gate_block, up_block = weights[0], weights[1]
    gate_value = jnp.dot(all_tokens, gate_block, preferred_element_type=jnp.float32)
    up_value = jnp.dot(all_tokens, up_block, preferred_element_type=jnp.float32)
    hidden_grad = contract_last(all_cotangent, down_weight)
    parts = jnp.stack((gate_value, up_value, hidden_grad)).astype(jnp.bfloat16)
    rows, columns = gate_value.shape
    parts = parts.reshape(3, n_inp, rows // n_inp, columns)
    parts = lax.all_to_all(parts, "inp", split_axis=1, concat_axis=1, tiled=True)
    sums = jnp.sum(parts.astype(jnp.float32), axis=1)
    shares = jnp.stack(local_step(sums[0], sums[1], sums[2]))
    full = lax.all_gather(shares, "inp", axis=1, tiled=True)
    hidden, gate_grad, up_grad = full[0], full[1], full[2]
    input_terms = contract_last(gate_grad, gate_block) + contract_last(up_grad, up_block)
    token_grad = lax.psum_scatter(input_terms, ("dep", "out"), scatter_dimension=0, tiled=True)
    grads = jnp.stack(
        (contract_first(all_tokens, gate_grad), contract_first(all_tokens, up_grad))
    ).astype(jnp.bfloat16)
    grads = lax.all_to_all(grads, "dep", split_axis=1, concat_axis=2, tiled=True)
    grads = grads.astype(jnp.float32)
    down_total = contract_first(hidden, all_cotangent)
    return (token_grad, grads[0], grads[1], down_total)


def solution(mesh):
    return jax.shard_map(
        shards,
        mesh=mesh,
        in_specs=(
            P(("dep", "out"), "inp"),
            P(("dep", "out"), "inp"),
            P(("inp", "dep"), "out"),
            P(("inp", "dep"), "out"),
            P(("out", "dep"), "inp"),
        ),
        out_specs=(
            P(("dep", "out"), "inp"),
            P(("inp", "dep"), "out"),
            P(("inp", "dep"), "out"),
            P(("out", "dep"), "inp"),
        ),
        check_vma=False,
    )
```

```python
import jax
import jax.numpy as jnp
from jax import lax
from jax.experimental import pallas as pl
from jax.experimental.pallas import tpu as pltpu
from jax.sharding import PartitionSpec as P

F32, BF16 = jnp.float32, jnp.bfloat16
MESH = pl.DeviceIdType.MESH
NX, NY, NZH = 4, 4, 4
SUB = 112
HALF = 512
COPIES = 160


def nt(left_side, right_side):
    return lax.dot_general(left_side, right_side, (((1,), (1,)), ((), ())), preferred_element_type=F32)


def nn(left_side, right_side):
    return jnp.dot(left_side, right_side, preferred_element_type=F32)


def tn(left_side, right_side):
    return lax.dot_general(left_side, right_side, (((0,), (0,)), ((), ())), preferred_element_type=F32)


def local_step(gate_value, up_value, hidden_grad):
    logistic = 1.0 / (1.0 + jnp.exp(-gate_value))
    activated = gate_value * logistic
    hidden = (activated * up_value).astype(BF16)
    up_grad = (hidden_grad * activated).astype(BF16)
    gate_grad = (hidden_grad * up_value * logistic * (1.0 + gate_value * (1.0 - logistic))).astype(BF16)
    return (hidden, gate_grad, up_grad)


def lanes(block):
    return pl.ds(pl.multiple_of(block * 128, 128), 128)


def kernel(
    tok_in, cot_in, gate_in, up_in, down_in,
    tg_out, gate_out, up_out, down_out,
    wt, wblk, gu, tok, cot, rs_send, rs_recv, hg_send, hg_recv, hz_send, hz_recv,
    grads, hid, wg_send, wg_recv, ta_send, ta_recv, tb_send, tb_recv, tc_send, tc_recv, td_send, td_recv,
    send_sems, recv_sems,
):
    inp, y, dep = lax.axis_index("inp"), lax.axis_index("out"), lax.axis_index("dep")
    zl, x = inp // NX, inp % NX
    zh, c = dep // 2, dep % 2
    z = zh * 2 + zl

    def at(x_=x, y_=y, zh_=zh, zl_=zl, c_=c):
        return (zl_ * NX + x_, y_, zh_ * 2 + c_)

    def ring(step):
        there = (z + step + 8) % 8
        return (there // 2, there % 2)

    xs = [(x + k) % NX for k in range(NX)]
    ys = [(y + k) % NY for k in range(NY)]
    zhs = [(zh + k) % NZH for k in range(NZH)]
    cs = [c, 1 - c]
    sides = [ring(1), ring(-1)]
    around = [at(zh_=side[0], zl_=side[1]) for side in sides]
    partner = at(zl_=1 - zl)

    peers = [at(c_=cs[1])]
    peers += [at(x_=xs[k], c_=cs[e]) for k in range(1, NX) for e in range(2)]
    peers += [at(x_=xs[k], zh_=zhs[m]) for k in range(NX) for m in range(1, NZH)]
    peers += [at(y_=ys[k]) for k in range(1, NY)]
    peers += around
    barrier = pltpu.get_barrier_semaphore()
    for peer in peers:
        pl.semaphore_signal(barrier, inc=1, device_id=peer, device_id_type=MESH)

    for q in range(NZH):
        columns = pl.ds(q * 896, 896)
        both = jnp.concatenate((gate_in[:, columns], up_in[:, columns]), axis=0)
        wt[q] = both.T.reshape(2, NX, SUB, 128)
    wblk[x * 2 + c] = wt[:, c, x]
    tok[zh, c, y, :, lanes(x)] = tok_in[:, lanes(zh)]
    cot[zh, c, y] = cot_in[...]

    pl.semaphore_wait(barrier, len(peers))

    started = []

    def send(src, dst, device):
        index = len(started)
        copy = pltpu.make_async_remote_copy(
            src_ref=src, dst_ref=dst, send_sem=send_sems.at[index], recv_sem=recv_sems.at[index],
            device_id=device, device_id_type=MESH,
        )
        copy.start()
        started.append(copy)
        return copy

    def arrive(copies):
        for copy in copies:
            copy.wait_recv()

    tok_first = [
        send(tok_in.at[:, lanes(zhs[m])], tok.at[zh, c, y, :, lanes(x)], at(x_=xs[k], zh_=zhs[m]))
        for m in range(NZH) for k in range(NX) if (m, k) != (0, 0)
    ]
    cot_first = [send(cot_in, cot.at[zh, c, y], at(zh_=zhs[m])) for m in range(1, NZH)]
    order = [zhs[2], zhs[1], zhs[3], zhs[0]]
    weights = [
        [
            send(wt.at[q, cs[e], xs[k]], wblk.at[x * 2 + c, q], at(x_=xs[k], c_=cs[e]))
            for k in range(NX) for e in range(2) if (k, e) != (0, 0)
        ]
        for q in order
    ]

    def spread(buffer, first):
        arrive(first)
        own = buffer.at[:, c, y]
        return [send(own, own, at(y_=ys[k])) for k in range(1, NY)], [send(own, own, at(c_=cs[1]))]

    def share(buffer, by_y, by_core):
        for k in range(1, NY):
            by_y[k - 1].wait_recv()
            rows = buffer.at[:, c, ys[NY - k]]
            by_core.append(send(rows, rows, at(c_=cs[1])))

    tok_y, tok_core = spread(tok, tok_first)
    cot_y, cot_core = spread(cot, cot_first)

    def assemble(q, copies):
        arrive(copies)
        for k in range(NX):
            even, odd = wblk[2 * k, q], wblk[2 * k + 1, q]
            here = pl.ds(k * 128, 128)
            gu[0, q, :, here] = jnp.concatenate((even[:, :64], odd[:, :64]), axis=1)
            gu[1, q, :, here] = jnp.concatenate((even[:, 64:], odd[:, 64:]), axis=1)

    assemble(order[0], weights[0])
    share(tok, tok_y, tok_core)
    arrive(tok_core)

    def partial(there):
        rows = gu[:, there[0]].reshape(2 * SUB, HALF)
        seen = tok[pl.ds(there[1] * 2, 2)].reshape(HALF, HALF)
        return nt(rows, seen).reshape(2, SUB, HALF)

    halves = [pl.ds(0, 256), pl.ds(256, 256)]
    own = partial(ring(4))
    rs_send[:, 0] = jnp.stack((own, own)).astype(BF16)
    moving = [
        [send(rs_send.at[d, 0, m, :, halves[d]], rs_recv.at[d, 0, m, :, halves[d]], around[d]) for d in range(2)]
        for m in range(2)
    ]

    for q in range(1, NZH):
        assemble(order[q], weights[q])
    share(cot, cot_y, cot_core)

    def onward(step, moving):
        terms = [partial(ring(4 - step)), partial(ring(step - 4))]
        later = []
        for m in range(2):
            row = []
            for d in range(2):
                moving[m][d].wait_recv()
                if step == 1:
                    came = rs_recv[d, 0, m, :, halves[d]].astype(F32)
                    parts = [terms[d][m][:, :256], terms[d][m][:, 256:]]
                    parts[d] = parts[d] + came
                    total = jnp.concatenate(parts, axis=1)
                else:
                    total = terms[d][m] + rs_recv[d, step - 1, m].astype(F32)
                rs_send[d, step, m] = total.astype(BF16)
                row.append(send(rs_send.at[d, step, m], rs_recv.at[d, step, m], around[d]))
            later.append(row)
        return later

    moving = onward(1, moving)

    arrive(cot_core)
    all_cot = cot[...].reshape(2 * HALF, HALF)

    def hidden_part(q):
        rows = down_in[pl.ds(pl.multiple_of(q * SUB, 16), SUB), :]
        return nt(rows, all_cot)

    by_x = []
    for k in range(1, NX):
        part = hidden_part(xs[k]).astype(BF16)
        hg_send[k - 1, 0] = part[:, :HALF]
        hg_send[k - 1, 1] = part[:, HALF:]
        by_x.append(send(hg_send.at[k - 1], hg_recv.at[k - 1], at(x_=xs[k])))
    moving = onward(2, moving)
    own = hidden_part(x)
    hz_send[0] = own[:, :HALF]
    hz_send[1] = own[:, HALF:]
    arrive(by_x)

    def hidden_sum(half):
        total = hz_send[half]
        for k in range(NX - 1):
            total = total + hg_recv[k, half].astype(F32)
        return total

    hz_recv[0] = hidden_sum(1 - zl).astype(BF16)
    by_pair = send(hz_recv.at[0], hz_recv.at[1], partner)
    moving = onward(3, moving)
    hidden_grad = hidden_sum(zl)
    by_pair.wait_recv()
    hidden_grad = hidden_grad + hz_recv[1].astype(F32)
    values = partial((zh, zl))
    sums = []
    for m in range(2):
        total = values[m]
        for d in range(2):
            moving[m][d].wait_recv()
            total = total + rs_recv[d, 3, m].astype(F32)
        sums.append(total)
    hidden, gate_grad, up_grad = local_step(sums[0], sums[1], hidden_grad)

    grads[zl, 0, zh] = gate_grad
    grads[zl, 1, zh] = up_grad

    def chunk(there, m, step, d):
        if step == 3:
            return grads.at[there[1], m, there[0], :, halves[d]]
        return grads.at[there[1], m, there[0]]

    def forward(step):
        rows = []
        for m in range(2):
            row = []
            for d in range(2):
                block = chunk(ring(-step if d == 0 else step), m, step, d)
                row.append(send(block, block, around[d]))
            rows.append(row)
        return rows

    moving = forward(0)
    hid[zl, x] = hidden
    by_pair = send(hid.at[zl, x], hid.at[zl, x], partner)
    by_pair.wait_recv()
    by_x = [send(hid.at[:, x], hid.at[:, x], at(x_=xs[k])) for k in range(1, NX)]

    returned = []

    def weight_grads(q):
        both = []
        for m in range(2):
            both.append(
                nn(grads[0, m, q], tok[0:2].reshape(HALF, HALF))
                + nn(grads[1, m, q], tok[2:4].reshape(HALF, HALF))
            )
        both = [one.astype(BF16) for one in both]
        for k in range(NX):
            here = [one[:, k * 128 : (k + 1) * 128] for one in both]
            wg_send[q, 0, k] = jnp.concatenate((here[0][:, :64], here[1][:, :64]), axis=1)
            wg_send[q, 1, k] = jnp.concatenate((here[0][:, 64:], here[1][:, 64:]), axis=1)
        wg_recv[q, c, x] = wg_send[q, c, x]
        for k in range(NX):
            for e in range(2):
                if (k, e) != (0, 0):
                    returned.append(
                        send(wg_send.at[q, cs[e], xs[k]], wg_recv.at[q, c, x], at(x_=xs[k], c_=cs[e]))
                    )

    turn = 2 * zl - 1
    finished = [zh, (zh + turn + NZH) % NZH, (zh - turn + NZH) % NZH, zhs[2]]
    for step in range(4):
        later = []
        for m in range(2):
            arrive(moving[m])
            if step < 3:
                row = []
                for d in range(2):
                    block = chunk(ring(-step - 1 if d == 0 else step + 1), m, step + 1, d)
                    row.append(send(block, block, around[d]))
                later.append(row)
        moving = later
        if step < 3:
            weight_grads(finished[step])
        if step == 1:
            arrive(by_x)
            for q in range(NX):
                down_out[pl.ds(q * SUB, SUB), :] = nn(
                    hid[0, q], cot[0:2].reshape(HALF, HALF)
                ) + nn(hid[1, q], cot[2:4].reshape(HALF, HALF))

    terms = []
    for half in range(2):
        term = tn(grads[half].reshape(8 * SUB, HALF), gu[...].reshape(8 * SUB, HALF))
        terms.append(term.reshape(2, 2, NY, 32, HALF))
    ta_all = jnp.concatenate(terms, axis=0)
    tb_send[...] = ta_all
    ta_send[...] = tb_send[:, cs[1]].astype(BF16)
    by_core = send(ta_send, ta_recv, at(c_=cs[1]))
    weight_grads(finished[3])
    by_core.wait_recv()
    ta_send_sum = tb_send[:, c] + ta_recv[...].astype(F32)
    tb_send[:, c] = ta_send_sum
    for k in range(NX):
        tb_recv[0, k] = ta_send_sum[:, :, :, k * 128 : (k + 1) * 128].astype(BF16)
    by_x = [send(tb_recv.at[0, xs[k]], tb_recv.at[1, k], at(x_=xs[k])) for k in range(1, NX)]
    total = tb_send[:, c, :, :, lanes(x)]
    arrive(by_x)
    for k in range(1, NX):
        total = total + tb_recv[1, k].astype(F32)
    tc_send[...] = total
    for k in range(NY):
        tc_recv[0, k] = total[:, k].astype(BF16)
    by_y = [send(tc_recv.at[0, ys[k]], tc_recv.at[1, k], at(y_=ys[k])) for k in range(1, NY)]
    total = tc_send[:, y]
    arrive(by_y)
    for k in range(1, NY):
        total = total + tc_recv[1, k].astype(F32)
    td_send[...] = total
    td_recv[zh] = td_send[zh]
    by_z = [send(td_send.at[zhs[m]], td_recv.at[zh], at(zh_=zhs[m])) for m in range(1, NZH)]

    arrive(returned)
    for q in range(NZH):
        block = wg_recv[q].reshape(896, 128).T.astype(F32)
        gate_out[:, pl.ds(q * 896, 896)] = block[:64]
        up_out[:, pl.ds(q * 896, 896)] = block[64:]
    arrive(by_z)
    for q in range(NZH):
        tg_out[:, pl.ds(q * 128, 128)] = td_recv[q]
    for copy in started:
        copy.wait_send()


def shards(tokens, cotangent, gate_weight, up_weight, down_weight):
    vmem = pl.BlockSpec(memory_space=pltpu.VMEM)
    outs = [
        jax.ShapeDtypeStruct(tokens.shape, F32),
        jax.ShapeDtypeStruct(gate_weight.shape, F32),
        jax.ShapeDtypeStruct(up_weight.shape, F32),
        jax.ShapeDtypeStruct(down_weight.shape, F32),
    ]
    scratch = [
        pltpu.VMEM((NZH, 2, NX, SUB, 128), BF16),
        pltpu.VMEM((2 * NX, NZH, SUB, 128), BF16),
        pltpu.VMEM((2, NZH, SUB, HALF), BF16),
        pltpu.VMEM((NZH, 2, NY, 32, HALF), BF16),
        pltpu.VMEM((NZH, 2, NY, 32, HALF), BF16),
        pltpu.VMEM((2, 4, 2, SUB, HALF), BF16),
        pltpu.VMEM((2, 4, 2, SUB, HALF), BF16),
        pltpu.VMEM((NX - 1, 2, SUB, HALF), BF16),
        pltpu.VMEM((NX - 1, 2, SUB, HALF), BF16),
        pltpu.VMEM((2, SUB, HALF), F32),
        pltpu.VMEM((2, SUB, HALF), BF16),
        pltpu.VMEM((2, 2, NZH, SUB, HALF), BF16),
        pltpu.VMEM((2, NX, SUB, HALF), BF16),
        pltpu.VMEM((NZH, 2, NX, SUB, 128), BF16),
        pltpu.VMEM((NZH, 2, NX, SUB, 128), BF16),
        pltpu.VMEM((NZH, NY, 32, HALF), BF16),
        pltpu.VMEM((NZH, NY, 32, HALF), BF16),
        pltpu.VMEM((NZH, 2, NY, 32, HALF), F32),
        pltpu.VMEM((2, NX, NZH, NY, 32, 128), BF16),
        pltpu.VMEM((NZH, NY, 32, 128), F32),
        pltpu.VMEM((2, NY, NZH, 32, 128), BF16),
        pltpu.VMEM((NZH, 32, 128), F32),
        pltpu.VMEM((NZH, 32, 128), F32),
        pltpu.SemaphoreType.DMA((COPIES,)),
        pltpu.SemaphoreType.DMA((COPIES,)),
    ]
    return pl.pallas_call(
        kernel,
        out_shape=outs,
        in_specs=[vmem] * 5,
        out_specs=[vmem] * 4,
        scratch_shapes=scratch,
        compiler_params=pltpu.CompilerParams(
            collective_id=0, has_side_effects=True, vmem_limit_bytes=52 * 2**20
        ),
        name="layer",
    )(tokens, cotangent, gate_weight, up_weight, down_weight)


def solution(mesh):
    return jax.shard_map(
        shards,
        mesh=mesh,
        in_specs=(
            P(("dep", "out"), "inp"),
            P(("dep", "out"), "inp"),
            P(("inp", "dep"), "out"),
            P(("inp", "dep"), "out"),
            P(("out", "dep"), "inp"),
        ),
        out_specs=(
            P(("dep", "out"), "inp"),
            P(("inp", "dep"), "out"),
            P(("inp", "dep"), "out"),
            P(("out", "dep"), "inp"),
        ),
        check_vma=False,
    )
```

```python
import jax
import jax.numpy as jnp
from jax import lax
from jax.experimental import pallas as pl
from jax.experimental.pallas import tpu as pltpu
from jax.sharding import PartitionSpec as P

F32, BF16 = jnp.float32, jnp.bfloat16
MESH = pl.DeviceIdType.MESH
NX, NY, NZH = 4, 4, 4
SUB = 112
HALF = 512
COPIES = 160


def nt(left_side, right_side):
    return lax.dot_general(left_side, right_side, (((1,), (1,)), ((), ())), preferred_element_type=F32)


def nn(left_side, right_side):
    return jnp.dot(left_side, right_side, preferred_element_type=F32)


def tn(left_side, right_side):
    return lax.dot_general(left_side, right_side, (((0,), (0,)), ((), ())), preferred_element_type=F32)


def local_step(gate_value, up_value, hidden_grad):
    logistic = 1.0 / (1.0 + jnp.exp(-gate_value))
    activated = gate_value * logistic
    hidden = (activated * up_value).astype(BF16)
    up_grad = (hidden_grad * activated).astype(BF16)
    gate_grad = (hidden_grad * up_value * logistic * (1.0 + gate_value * (1.0 - logistic))).astype(BF16)
    return (hidden, gate_grad, up_grad)


def lanes(block):
    return pl.ds(pl.multiple_of(block * 128, 128), 128)


def kernel(
    tok_hbm, cot_hbm, gate_hbm, up_hbm, down_hbm,
    tg_out, wg_out, down_out,
    tok_in, cot_in, gate_in, up_in, down_in,
    wt, wblk, gu, tok, cot, rs_send, rs_recv, hg_send, hg_recv, hg_own, pair,
    grads, hid, wg_send, wg_recv, part, ta_send, ta_recv, tb_send, tb_recv, tc_send, tc_recv,
    load_sems, send_sems, recv_sems,
):
    inp, y, dep = lax.axis_index("inp"), lax.axis_index("out"), lax.axis_index("dep")
    zl, x = inp // NX, inp % NX
    zh, c = dep // 2, dep % 2
    z = zh * 2 + zl

    def at(x_=x, y_=y, zh_=zh, zl_=zl, c_=c):
        return (zl_ * NX + x_, y_, zh_ * 2 + c_)

    def ring(step):
        there = (z + step + 8) % 8
        return (there // 2, there % 2)

    xs = [(x + k) % NX for k in range(NX)]
    ys = [(y + k) % NY for k in range(NY)]
    zhs = [(zh + k) % NZH for k in range(NZH)]
    cs = [c, 1 - c]
    sides = [ring(1), ring(-1)]
    around = [at(zh_=side[0], zl_=side[1]) for side in sides]
    partner = at(zl_=1 - zl)

    loads = []
    for src, dst in (
        (gate_hbm, gate_in), (up_hbm, up_in), (tok_hbm, tok_in), (cot_hbm, cot_in), (down_hbm, down_in)
    ):
        loads.append(pltpu.make_async_copy(src, dst, load_sems.at[len(loads)]))
        loads[-1].start()

    peers = [at(zh_=zhs[m], y_=ys[k]) for m in range(1, NZH) for k in range(NY)]
    peers += [at(x_=xs[k], zh_=zhs[m]) for m in range(1, NZH) for k in range(1, NX)]
    peers += around
    peers += [at(y_=ys[k]) for k in range(1, NY)]
    peers += [at(x_=xs[k], c_=cs[e]) for k in range(1, NX) for e in range(2)]
    peers += [at(c_=cs[1])]
    barrier = pltpu.get_barrier_semaphore()
    for peer in peers:
        pl.semaphore_signal(barrier, inc=1, device_id=peer, device_id_type=MESH)

    for load in loads:
        load.wait()

    for q in range(NZH):
        columns = pl.ds(q * 896, 896)
        both = jnp.concatenate((gate_in[:, columns], up_in[:, columns]), axis=0)
        wt[q] = both.T.reshape(2, NX, SUB, 128)
    wblk[x * 2 + c] = wt[:, c, x]
    tok[zh, c, y, :, lanes(x)] = tok_in[:, lanes(zh)]
    cot[zh, c, y] = cot_in[...]

    pl.semaphore_wait(barrier, len(peers))

    started = []

    def send(src, dst, device):
        index = len(started)
        copy = pltpu.make_async_remote_copy(
            src_ref=src, dst_ref=dst, send_sem=send_sems.at[index], recv_sem=recv_sems.at[index],
            device_id=device, device_id_type=MESH,
        )
        copy.start()
        started.append(copy)
        return copy

    def arrive(copies):
        for copy in copies:
            copy.wait_recv()

    tok_first = [
        send(tok_in.at[:, lanes(zhs[m])], tok.at[zh, c, y, :, lanes(x)], at(x_=xs[k], zh_=zhs[m]))
        for m in (2, 1, 3, 0) for k in (2, 1, 3, 0) if (m, k) != (0, 0)
    ]
    cot_first = [send(cot_in, cot.at[zh, c, y], at(zh_=zhs[m])) for m in (2, 1, 3)]

    def send_weights(q):
        return [
            send(wt.at[q, cs[e], xs[k]], wblk.at[x * 2 + c, q], at(x_=xs[k], c_=cs[e]))
            for k in (2, 1, 3, 0) for e in range(2) if (k, e) != (0, 0)
        ]

    def spread(buffer, first):
        arrive(first)
        own = buffer.at[:, c, y]
        return {k: send(own, own, at(y_=ys[k])) for k in (2, 1, 3)}, [send(own, own, at(c_=cs[1]))]

    def share(buffer, by_y, by_core):
        for k in (1, 3, 2):
            by_y[k].wait_recv()
            rows = buffer.at[:, c, ys[NY - k]]
            by_core.append(send(rows, rows, at(c_=cs[1])))

    order = [zhs[2], zhs[1], zhs[3], zhs[0]]
    weights = [send_weights(order[0])]
    tok_y, tok_core = spread(tok, tok_first)
    cot_y, cot_core = spread(cot, cot_first)
    for q in range(1, NZH):
        weights.append(send_weights(order[q]))

    def assemble(q):
        arrive(weights[q])
        for k in range(NX):
            even, odd = wblk[2 * k, order[q]], wblk[2 * k + 1, order[q]]
            here = pl.ds(k * 128, 128)
            gu[0, order[q], :, here] = jnp.concatenate((even[:, :64], odd[:, :64]), axis=1)
            gu[1, order[q], :, here] = jnp.concatenate((even[:, 64:], odd[:, 64:]), axis=1)

    assemble(0)
    share(tok, tok_y, tok_core)
    arrive(tok_core)

    def partial(there):
        rows = gu[:, there[0]].reshape(2 * SUB, HALF)
        seen = tok[pl.ds(there[1] * 2, 2)].reshape(HALF, HALF)
        return nt(rows, seen).reshape(2, SUB, HALF)

    halves = [pl.ds(0, 256), pl.ds(256, 256)]
    own = partial(ring(4)).astype(BF16)
    rs_send[0, 0] = own
    rs_send[1, 0] = own
    moving = [
        [send(rs_send.at[d, 0, m, :, halves[d]], rs_recv.at[d, 0, m, :, halves[d]], around[d]) for d in range(2)]
        for m in range(2)
    ]
    assemble(1)
    assemble(2)

    share(cot, cot_y, cot_core)
    arrive(cot_core)

    def hidden_part(q):
        rows = down_in[pl.ds(pl.multiple_of(q * SUB, 16), SUB), :]
        return nt(rows, cot[...].reshape(2 * HALF, HALF))

    by_x = []
    for k in (2, 1, 3):
        some = hidden_part(xs[k]).astype(BF16)
        hg_send[k - 1, 0] = some[:, :HALF]
        hg_send[k - 1, 1] = some[:, HALF:]
        by_x.append(send(hg_send.at[k - 1], hg_recv.at[k - 1], at(x_=xs[k])))

    def onward(step, moving):
        terms = [partial(ring(4 - step)), partial(ring(step - 4))]
        later = []
        for m in range(2):
            row = []
            for d in range(2):
                moving[m][d].wait_recv()
                if step == 1:
                    came = rs_recv[d, 0, m, :, halves[d]].astype(F32)
                    sides = [terms[d][m][:, :256], terms[d][m][:, 256:]]
                    sides[d] = sides[d] + came
                    total = jnp.concatenate(sides, axis=1)
                else:
                    total = terms[d][m] + rs_recv[d, step - 1, m].astype(F32)
                rs_send[d, step, m] = total.astype(BF16)
                row.append(send(rs_send.at[d, step, m], rs_recv.at[d, step, m], around[d]))
            later.append(row)
        return later

    moving = onward(1, moving)
    assemble(3)
    some = hidden_part(x)
    hg_own[0] = some[:, :HALF]
    hg_own[1] = some[:, HALF:]
    moving = onward(2, moving)

    def hidden_sum(half):
        total = hg_own[half]
        for k in range(NX - 1):
            total = total + hg_recv[k, half].astype(F32)
        return total

    arrive(by_x)
    pair[0] = hidden_sum(1 - zl).astype(BF16)
    by_pair = send(pair.at[0], pair.at[1], partner)
    moving = onward(3, moving)
    hidden_grad = hidden_sum(zl)
    values = partial((zh, zl))
    by_pair.wait_recv()
    hidden_grad = hidden_grad + pair[1].astype(F32)
    sums = []
    for m in range(2):
        total = values[m]
        for d in range(2):
            moving[m][d].wait_recv()
            total = total + rs_recv[d, 3, m].astype(F32)
        sums.append(total)
    hidden, gate_grad, up_grad = local_step(sums[0], sums[1], hidden_grad)

    grads[zl, 0, zh] = gate_grad
    grads[zl, 1, zh] = up_grad

    def chunk(there, m, step, d):
        if step == 3:
            return grads.at[there[1], m, there[0], :, halves[d]]
        return grads.at[there[1], m, there[0]]

    def forward(step, m):
        row = []
        for d in range(2):
            block = chunk(ring(-step if d == 0 else step), m, step, d)
            row.append(send(block, block, around[d]))
        return row

    moving = [forward(0, m) for m in range(2)]
    hid[zl, x] = hidden
    by_pair = send(hid.at[zl, x], hid.at[zl, x], partner)

    returned = []

    def weight_grads(q):
        both = nn(grads[0, :, q].reshape(2 * SUB, HALF), tok[0:2].reshape(HALF, HALF))
        both = both + nn(grads[1, :, q].reshape(2 * SUB, HALF), tok[2:4].reshape(HALF, HALF))
        both = both.astype(BF16)
        for k in range(NX):
            here = both[:, k * 128 : (k + 1) * 128]
            wg_send[q, 0, k] = jnp.concatenate((here[:SUB, :64], here[SUB:, :64]), axis=1)
            wg_send[q, 1, k] = jnp.concatenate((here[:SUB, 64:], here[SUB:, 64:]), axis=1)
        wg_recv[q, c, x] = wg_send[q, c, x]
        for k in (2, 1, 3, 0):
            for e in range(2):
                if (k, e) != (0, 0):
                    returned.append(
                        send(wg_send.at[q, cs[e], xs[k]], wg_recv.at[q, c, x], at(x_=xs[k], c_=cs[e]))
                    )

    def over_core(p, half):
        term = tn(grads[half].reshape(8 * SUB, HALF), gu[...].reshape(8 * SUB, HALF))
        part[p] = term.reshape(2, 2, NY, 32, HALF)
        ta_send[p] = part[p, :, cs[1]].astype(BF16)
        return send(ta_send.at[p], ta_recv.at[p], at(c_=cs[1]))

    def over_x(p, by_core):
        by_core.wait_recv()
        total = part[p, :, c] + ta_recv[p].astype(F32)
        part[p, :, c] = total
        for k in range(NX):
            tb_send[p, k] = total[:, :, :, k * 128 : (k + 1) * 128].astype(BF16)
        return [send(tb_send.at[p, xs[k]], tb_recv.at[p, k - 1], at(x_=xs[k])) for k in (2, 1, 3)]

    def sum_x(p, half, by_x):
        arrive(by_x)
        total = part[p, :, c, :, :, lanes(x)]
        for k in range(NX - 1):
            total = total + tb_recv[p, k].astype(F32)
        tc_send[pl.ds(half * 2, 2)] = total.astype(BF16)

    turn = 2 * zl - 1
    finished = [zh, (zh + turn + NZH) % NZH, (zh - turn + NZH) % NZH, zhs[2]]
    for step in range(4):
        later = []
        for m in range(2):
            arrive(moving[m])
            if step < 3:
                later.append(forward(step + 1, m))
        moving = later
        if step == 0:
            by_pair.wait_recv()
            by_x = [send(hid.at[:, x], hid.at[:, x], at(x_=xs[k])) for k in (2, 1, 3)]
        if step == 2:
            early = over_x(0, over_core(0, 1 - zl))
        if step < 2:
            weight_grads(finished[step])
    by_core = over_core(1, zl)
    sum_x(0, 1 - zl, early)
    late = over_x(1, by_core)
    weight_grads(finished[2])
    weight_grads(finished[3])
    sum_x(1, zl, late)
    by_place = [
        send(tc_send.at[zhs[m], ys[k]], tc_recv.at[zh, k], at(zh_=zhs[m], y_=ys[k]))
        for m in (2, 1, 3, 0) for k in (2, 1, 3, 0) if (m, k) != (0, 0)
    ]
    tc_recv[zh, 0] = tc_send[zh, y]
    arrive(by_x)
    down_out[...] = nn(hid[0].reshape(4 * SUB, HALF), cot[0:2].reshape(HALF, HALF)) + nn(
        hid[1].reshape(4 * SUB, HALF), cot[2:4].reshape(HALF, HALF)
    )
    arrive(returned)
    wg_out[...] = wg_recv[...].reshape(NZH, 896, 128)
    arrive(by_place)
    for q in range(NZH):
        total = tc_recv[q, 0].astype(F32)
        for k in range(1, NY):
            total = total + tc_recv[q, k].astype(F32)
        tg_out[:, pl.ds(q * 128, 128)] = total
    for copy in started:
        copy.wait_send()


def finish(tg_in, wg_in, down_in, tg_out, gate_out, up_out, down_out):
    for q in range(NZH):
        block = wg_in[q].T.astype(F32)
        gate_out[:, pl.ds(q * 896, 896)] = block[:64]
        up_out[:, pl.ds(q * 896, 896)] = block[64:]
    down_out[...] = down_in[...]
    tg_out[...] = tg_in[...]


def shards(tokens, cotangent, gate_weight, up_weight, down_weight):
    vmem = pl.BlockSpec(memory_space=pltpu.VMEM)
    hbm = pl.BlockSpec(memory_space=pltpu.HBM)
    outs = [
        jax.ShapeDtypeStruct(tokens.shape, F32),
        jax.ShapeDtypeStruct(gate_weight.shape, F32),
        jax.ShapeDtypeStruct(up_weight.shape, F32),
        jax.ShapeDtypeStruct(down_weight.shape, F32),
    ]
    between = [
        outs[0],
        jax.ShapeDtypeStruct((NZH, 896, 128), BF16),
        outs[3],
    ]
    scratch = [
        pltpu.VMEM(tokens.shape, BF16),
        pltpu.VMEM(cotangent.shape, BF16),
        pltpu.VMEM(gate_weight.shape, BF16),
        pltpu.VMEM(up_weight.shape, BF16),
        pltpu.VMEM(down_weight.shape, BF16),
        pltpu.VMEM((NZH, 2, NX, SUB, 128), BF16),
        pltpu.VMEM((2 * NX, NZH, SUB, 128), BF16),
        pltpu.VMEM((2, NZH, SUB, HALF), BF16),
        pltpu.VMEM((NZH, 2, NY, 32, HALF), BF16),
        pltpu.VMEM((NZH, 2, NY, 32, HALF), BF16),
        pltpu.VMEM((2, 4, 2, SUB, HALF), BF16),
        pltpu.VMEM((2, 4, 2, SUB, HALF), BF16),
        pltpu.VMEM((NX - 1, 2, SUB, HALF), BF16),
        pltpu.VMEM((NX - 1, 2, SUB, HALF), BF16),
        pltpu.VMEM((2, SUB, HALF), F32),
        pltpu.VMEM((2, SUB, HALF), BF16),
        pltpu.VMEM((2, 2, NZH, SUB, HALF), BF16),
        pltpu.VMEM((2, NX, SUB, HALF), BF16),
        pltpu.VMEM((NZH, 2, NX, SUB, 128), BF16),
        pltpu.VMEM((NZH, 2, NX, SUB, 128), BF16),
        pltpu.VMEM((2, 2, 2, NY, 32, HALF), F32),
        pltpu.VMEM((2, 2, NY, 32, HALF), BF16),
        pltpu.VMEM((2, 2, NY, 32, HALF), BF16),
        pltpu.VMEM((2, NX, 2, NY, 32, 128), BF16),
        pltpu.VMEM((2, NX - 1, 2, NY, 32, 128), BF16),
        pltpu.VMEM((NZH, NY, 32, 128), BF16),
        pltpu.VMEM((NZH, NY, 32, 128), BF16),
        pltpu.SemaphoreType.DMA((5,)),
        pltpu.SemaphoreType.DMA((COPIES,)),
        pltpu.SemaphoreType.DMA((COPIES,)),
    ]
    token_grad, weight_grad, down_grad = pl.pallas_call(
        kernel,
        out_shape=between,
        in_specs=[hbm] * 5,
        out_specs=[vmem] * 3,
        scratch_shapes=scratch,
        compiler_params=pltpu.CompilerParams(
            collective_id=0, has_side_effects=True, vmem_limit_bytes=60 * 2**20
        ),
        name="layer",
    )(tokens, cotangent, gate_weight, up_weight, down_weight)
    return pl.pallas_call(
        finish,
        out_shape=outs,
        in_specs=[vmem] * 3,
        out_specs=[vmem] * 4,
        compiler_params=pltpu.CompilerParams(vmem_limit_bytes=60 * 2**20),
        name="finish",
    )(token_grad, weight_grad, down_grad)


def solution(mesh):
    return jax.shard_map(
        shards,
        mesh=mesh,
        in_specs=(
            P(("dep", "out"), "inp"),
            P(("dep", "out"), "inp"),
            P(("inp", "dep"), "out"),
            P(("inp", "dep"), "out"),
            P(("out", "dep"), "inp"),
        ),
        out_specs=(
            P(("dep", "out"), "inp"),
            P(("inp", "dep"), "out"),
            P(("inp", "dep"), "out"),
            P(("out", "dep"), "inp"),
        ),
        check_vma=False,
    )
```

```python
import jax
import jax.numpy as jnp
from jax import lax
from jax.experimental import pallas as pl
from jax.experimental.pallas import tpu as pltpu
from jax.sharding import PartitionSpec as P

F32, BF16 = jnp.float32, jnp.bfloat16
MESH = pl.DeviceIdType.MESH
NX, NY, NZH = 4, 4, 4
SUB = 112
HALF = 512
PHASE = 256
COPIES = 180


def nt(left_side, right_side):
    return lax.dot_general(left_side, right_side, (((1,), (1,)), ((), ())), preferred_element_type=F32)


def nn(left_side, right_side):
    return jnp.dot(left_side, right_side, preferred_element_type=F32)


def tn(left_side, right_side):
    return lax.dot_general(left_side, right_side, (((0,), (0,)), ((), ())), preferred_element_type=F32)


def local_step(gate_value, up_value, hidden_grad):
    logistic = 1.0 / (1.0 + jnp.exp(-gate_value))
    activated = gate_value * logistic
    hidden = (activated * up_value).astype(BF16)
    up_grad = (hidden_grad * activated).astype(BF16)
    gate_grad = (hidden_grad * up_value * logistic * (1.0 + gate_value * (1.0 - logistic))).astype(BF16)
    return (hidden, gate_grad, up_grad)


def lanes(block):
    return pl.ds(pl.multiple_of(block * 128, 128), 128)


def kernel(
    tok_hbm, cot_hbm, gate_hbm, up_hbm, down_hbm,
    tg_out, wg_out, down_out,
    tok_in, cot_in, gate_in, up_in, down_in,
    wt, wblk, gu, tok, cot, rs_send, rs_recv, hg_send, hg_recv, hg_own, pair,
    grads, hid, wg_send, wg_recv, part, ta_send, ta_recv, tb_send, tb_recv, tc_send, tc_recv,
    load_sems, send_sems, recv_sems,
):
    inp, y, dep = lax.axis_index("inp"), lax.axis_index("out"), lax.axis_index("dep")
    zl, x = inp // NX, inp % NX
    zh, c = dep // 2, dep % 2
    z = zh * 2 + zl

    def at(x_=x, y_=y, zh_=zh, zl_=zl, c_=c):
        return (zl_ * NX + x_, y_, zh_ * 2 + c_)

    def ring(step):
        there = (z + step + 8) % 8
        return (there // 2, there % 2)

    xs = [(x + k) % NX for k in range(NX)]
    ys = [(y + k) % NY for k in range(NY)]
    zhs = [(zh + k) % NZH for k in range(NZH)]
    cs = [c, 1 - c]
    sides = [ring(1), ring(-1)]
    around = [at(zh_=side[0], zl_=side[1]) for side in sides]
    partner = at(zl_=1 - zl)

    loads = []
    for src, dst in (
        (gate_hbm, gate_in), (up_hbm, up_in), (tok_hbm, tok_in), (cot_hbm, cot_in), (down_hbm, down_in)
    ):
        loads.append(pltpu.make_async_copy(src, dst, load_sems.at[len(loads)]))
        loads[-1].start()

    peers = [at(zh_=zhs[m], y_=ys[k]) for m in range(1, NZH) for k in range(NY)]
    peers += [at(x_=xs[k], zh_=zhs[m]) for m in range(1, NZH) for k in range(1, NX)]
    peers += around
    peers += [at(y_=ys[k]) for k in range(1, NY)]
    peers += [at(x_=xs[k], c_=cs[e]) for k in range(1, NX) for e in range(2)]
    peers += [at(c_=cs[1])]
    barrier = pltpu.get_barrier_semaphore()
    for peer in peers:
        pl.semaphore_signal(barrier, inc=1, device_id=peer, device_id_type=MESH)

    for load in loads:
        load.wait()

    for q in range(NZH):
        columns = pl.ds(q * 896, 896)
        both = jnp.concatenate((gate_in[:, columns], up_in[:, columns]), axis=0)
        wt[q] = both.T.reshape(2, NX, SUB, 128)
    wblk[x * 2 + c] = wt[:, c, x]
    tok[zh // 2, zh % 2, c, y, :, lanes(x)] = tok_in[:, lanes(zh)]
    cot[zh // 2, zh % 2, c, y] = cot_in[...]

    pl.semaphore_wait(barrier, len(peers))

    started = []

    def send(src, dst, device):
        index = len(started)
        copy = pltpu.make_async_remote_copy(
            src_ref=src, dst_ref=dst, send_sem=send_sems.at[index], recv_sem=recv_sems.at[index],
            device_id=device, device_id_type=MESH,
        )
        copy.start()
        started.append(copy)
        return copy

    def arrive(copies):
        for copy in copies:
            copy.wait_recv()

    tok_first = [
        send(
            tok_in.at[:, lanes(zhs[m])],
            tok.at[zh // 2, zh % 2, c, y, :, lanes(x)],
            at(x_=xs[k], zh_=zhs[m]),
        )
        for m in (2, 1, 3, 0) for k in (2, 1, 3, 0) if (m, k) != (0, 0)
    ]
    cot_first = [send(cot_in, cot.at[zh // 2, zh % 2, c, y], at(zh_=zhs[m])) for m in (2, 1, 3)]

    def send_weights(q):
        return [
            send(wt.at[q, cs[e], xs[k]], wblk.at[x * 2 + c, q], at(x_=xs[k], c_=cs[e]))
            for k in (2, 1, 3, 0) for e in range(2) if (k, e) != (0, 0)
        ]

    def spread(buffer, p):
        own = buffer.at[:, p, c, y]
        return {k: send(own, own, at(y_=ys[k])) for k in (2, 1, 3)}, [send(own, own, at(c_=cs[1]))]

    def share(buffer, p, by_y, by_core):
        for k in (1, 3, 2):
            by_y[k].wait_recv()
            rows = buffer.at[:, p, c, ys[NY - k]]
            by_core.append(send(rows, rows, at(c_=cs[1])))
        arrive(by_core)

    order = [zhs[2], zhs[1], zhs[3], zhs[0]]
    weights = [send_weights(order[0])]
    arrive(tok_first)
    tok_later = [spread(tok, p) for p in range(2)]
    arrive(cot_first)
    cot_later = [spread(cot, p) for p in range(2)]
    for q in range(1, NZH):
        weights.append(send_weights(order[q]))

    def assemble(q):
        arrive(weights[q])
        for k in range(NX):
            even, odd = wblk[2 * k, order[q]], wblk[2 * k + 1, order[q]]
            here = pl.ds(k * 128, 128)
            gu[0, order[q], :, here] = jnp.concatenate((even[:, :64], odd[:, :64]), axis=1)
            gu[1, order[q], :, here] = jnp.concatenate((even[:, 64:], odd[:, 64:]), axis=1)

    def partial(there, p):
        rows = gu[:, there[0]].reshape(2 * SUB, HALF)
        return nt(rows, tok[there[1], p].reshape(PHASE, HALF)).reshape(2, SUB, PHASE)

    halves = [pl.ds(0, 128), pl.ds(128, 128)]

    def outset(p):
        own = partial(ring(4), p).astype(BF16)
        row = []
        for d in range(2):
            rs_send[p, d, 0, :, :, halves[d]] = own[:, :, d * 128 : (d + 1) * 128]
            row.append(
                send(rs_send.at[p, d, 0, :, :, halves[d]], rs_recv.at[p, d, 0, :, :, halves[d]], around[d])
            )
        return row

    def onward(step, p, row):
        terms = [partial(ring(4 - step), p), partial(ring(step - 4), p)]
        later = []
        for d in range(2):
            row[d].wait_recv()
            if step == 1:
                came = rs_recv[p, d, 0, :, :, halves[d]].astype(F32)
                two = [terms[d][:, :, :128], terms[d][:, :, 128:]]
                two[d] = two[d] + came
                total = jnp.concatenate(two, axis=2)
            else:
                total = terms[d] + rs_recv[p, d, step - 1].astype(F32)
            rs_send[p, d, step] = total.astype(BF16)
            later.append(send(rs_send.at[p, d, step], rs_recv.at[p, d, step], around[d]))
        return later

    def hidden_part(q, p):
        rows = down_in[pl.ds(pl.multiple_of(q * SUB, 16), SUB), :]
        return nt(rows, cot[:, p].reshape(2 * PHASE, HALF))

    def hidden_over_x(p):
        share(cot, p, *cot_later[p])
        copies = []
        for k in (2, 1, 3):
            some = hidden_part(xs[k], p).astype(BF16)
            for half in range(2):
                hg_send[p, k - 1, half] = some[:, half * PHASE : (half + 1) * PHASE]
            copies.append(send(hg_send.at[p, k - 1], hg_recv.at[p, k - 1], at(x_=xs[k])))
        some = hidden_part(x, p)
        for half in range(2):
            hg_own[p, half] = some[:, half * PHASE : (half + 1) * PHASE]
        return copies

    def hidden_sum(p, half):
        total = hg_own[p, half]
        for k in range(NX - 1):
            total = total + hg_recv[p, k, half].astype(F32)
        return total

    def hidden_pair(p, by_x):
        arrive(by_x)
        pair[p, 0] = hidden_sum(p, 1 - zl).astype(BF16)
        return send(pair.at[p, 0], pair.at[p, 1], partner)

    assemble(0)
    moving, by_x, by_pair = [None, None], [None, None], [None, None]
    for p in range(2):
        share(tok, p, *tok_later[p])
        moving[p] = outset(p)
    assemble(1)
    assemble(2)
    for p in range(2):
        moving[p] = onward(1, p, moving[p])
        by_x[p] = hidden_over_x(p)
    assemble(3)
    for p in range(2):
        moving[p] = onward(2, p, moving[p])
    by_pair[0] = hidden_pair(0, by_x[0])
    for p in range(2):
        moving[p] = onward(3, p, moving[p])
    by_pair[1] = hidden_pair(1, by_x[1])

    def chunk(there, p, step, d):
        if step == 3:
            return grads.at[there[1], p, :, there[0], :, halves[d]]
        return grads.at[there[1], p, :, there[0]]

    def forward(step, p):
        row = []
        for d in range(2):
            block = chunk(ring(-step if d == 0 else step), p, step, d)
            row.append(send(block, block, around[d]))
        return row

    for p in range(2):
        values = partial((zh, zl), p)
        hidden_grad = hidden_sum(p, zl)
        by_pair[p].wait_recv()
        hidden_grad = hidden_grad + pair[p, 1].astype(F32)
        for d in range(2):
            moving[p][d].wait_recv()
            values = values + rs_recv[p, d, 3].astype(F32)
        hidden, gate_grad, up_grad = local_step(values[0], values[1], hidden_grad)
        grads[zl, p, 0, zh] = gate_grad
        grads[zl, p, 1, zh] = up_grad
        moving[p] = forward(0, p)
        hid[zl, p, x] = hidden
        by_pair[p] = send(hid.at[zl, p, x], hid.at[zl, p, x], partner)

    returned = []

    def weight_grads(q):
        both = jnp.zeros((2 * SUB, HALF), F32)
        for half in range(2):
            for p in range(2):
                rows = grads[half, p, :, q].reshape(2 * SUB, PHASE)
                both = both + nn(rows, tok[half, p].reshape(PHASE, HALF))
        both = both.astype(BF16)
        for k in range(NX):
            here = both[:, k * 128 : (k + 1) * 128]
            wg_send[q, 0, k] = jnp.concatenate((here[:SUB, :64], here[SUB:, :64]), axis=1)
            wg_send[q, 1, k] = jnp.concatenate((here[:SUB, 64:], here[SUB:, 64:]), axis=1)
        wg_recv[q, c, x] = wg_send[q, c, x]
        for k in (2, 1, 3, 0):
            for e in range(2):
                if (k, e) != (0, 0):
                    returned.append(
                        send(wg_send.at[q, cs[e], xs[k]], wg_recv.at[q, c, x], at(x_=xs[k], c_=cs[e]))
                    )

    def over_core(p):
        for half in range(2):
            term = tn(grads[half, p].reshape(8 * SUB, PHASE), gu[...].reshape(8 * SUB, HALF))
            part[p, half] = term.reshape(2, NY, 32, HALF)
        ta_send[p] = part[p, :, cs[1]].astype(BF16)
        return send(ta_send.at[p], ta_recv.at[p], at(c_=cs[1]))

    def over_x(p, by_core):
        by_core.wait_recv()
        total = part[p, :, c] + ta_recv[p].astype(F32)
        part[p, :, c] = total
        for k in range(NX):
            tb_send[p, k] = total[:, :, :, k * 128 : (k + 1) * 128].astype(BF16)
        return [send(tb_send.at[p, xs[k]], tb_recv.at[p, k - 1], at(x_=xs[k])) for k in (2, 1, 3)]

    def sum_x(p, by_x):
        arrive(by_x)
        total = part[p, :, c, :, :, lanes(x)]
        for k in range(NX - 1):
            total = total + tb_recv[p, k].astype(F32)
        tc_send[:, p] = total.astype(BF16)

    turn = 2 * zl - 1
    finished = [zh, (zh + turn + NZH) % NZH, (zh - turn + NZH) % NZH, zhs[2]]
    for step in range(3):
        for p in range(2):
            arrive(moving[p])
            moving[p] = forward(step + 1, p)
            if step == 0:
                by_pair[p].wait_recv()
                by_x[p] = [send(hid.at[:, p, x], hid.at[:, p, x], at(x_=xs[k])) for k in (2, 1, 3)]
        if step < 2:
            weight_grads(finished[step])
    arrive(moving[0])
    early = over_x(0, over_core(0))
    arrive(moving[1])
    late = over_x(1, over_core(1))
    weight_grads(finished[2])
    weight_grads(finished[3])
    sum_x(0, early)
    sum_x(1, late)
    by_place = [
        send(
            tc_send.at[zhs[m] // 2, zhs[m] % 2, ys[k]], tc_recv.at[zh, k], at(zh_=zhs[m], y_=ys[k])
        )
        for m in (2, 1, 3, 0) for k in (2, 1, 3, 0) if (m, k) != (0, 0)
    ]
    tc_recv[zh, 0] = tc_send[zh // 2, zh % 2, y]
    arrive(by_x[0])
    arrive(by_x[1])
    down = jnp.zeros((4 * SUB, HALF), F32)
    for half in range(2):
        for p in range(2):
            rows = hid[half, p].reshape(4 * SUB, PHASE)
            down = down + nn(rows, cot[half, p].reshape(PHASE, HALF))
    down_out[...] = down
    arrive(returned)
    wg_out[...] = wg_recv[...].reshape(NZH, 896, 128)
    arrive(by_place)
    for q in range(NZH):
        total = tc_recv[q, 0].astype(F32)
        for k in range(1, NY):
            total = total + tc_recv[q, k].astype(F32)
        tg_out[:, pl.ds(q * 128, 128)] = total
    for copy in started:
        copy.wait_send()


def finish(tg_in, wg_in, down_in, tg_out, gate_out, up_out, down_out, tg, wg, down, gate, up, sems):
    loads = [pltpu.make_async_copy(wg_in.at[q], wg.at[q], sems.at[q]) for q in range(NZH)]
    loads.append(pltpu.make_async_copy(down_in, down, sems.at[NZH]))
    loads.append(pltpu.make_async_copy(tg_in, tg, sems.at[NZH + 1]))
    for load in loads:
        load.start()
    stores = []

    def store(src, dst):
        stores.append(pltpu.make_async_copy(src, dst, sems.at[len(loads) + len(stores)]))
        stores[-1].start()

    for q in range(NZH):
        loads[q].wait()
        here = pl.ds(q * 896, 896)
        block = wg[q].T.astype(F32)
        for rows, buffer, out in ((block[:64], gate, gate_out), (block[64:], up, up_out)):
            buffer[:, here] = rows
            store(buffer.at[:, here], out.at[:, here])
        if q == 1:
            loads[NZH].wait()
            store(down, down_out)
            loads[NZH + 1].wait()
            store(tg, tg_out)
    for copy in stores:
        copy.wait()


def shards(tokens, cotangent, gate_weight, up_weight, down_weight):
    vmem = pl.BlockSpec(memory_space=pltpu.VMEM)
    hbm = pl.BlockSpec(memory_space=pltpu.HBM)
    outs = [
        jax.ShapeDtypeStruct(tokens.shape, F32),
        jax.ShapeDtypeStruct(gate_weight.shape, F32),
        jax.ShapeDtypeStruct(up_weight.shape, F32),
        jax.ShapeDtypeStruct(down_weight.shape, F32),
    ]
    between = [
        outs[0],
        jax.ShapeDtypeStruct((NZH, 896, 128), BF16),
        outs[3],
    ]
    scratch = [
        pltpu.VMEM(tokens.shape, BF16),
        pltpu.VMEM(cotangent.shape, BF16),
        pltpu.VMEM(gate_weight.shape, BF16),
        pltpu.VMEM(up_weight.shape, BF16),
        pltpu.VMEM(down_weight.shape, BF16),
        pltpu.VMEM((NZH, 2, NX, SUB, 128), BF16),
        pltpu.VMEM((2 * NX, NZH, SUB, 128), BF16),
        pltpu.VMEM((2, NZH, SUB, HALF), BF16),
        pltpu.VMEM((2, 2, 2, NY, 32, HALF), BF16),
        pltpu.VMEM((2, 2, 2, NY, 32, HALF), BF16),
        pltpu.VMEM((2, 2, 4, 2, SUB, PHASE), BF16),
        pltpu.VMEM((2, 2, 4, 2, SUB, PHASE), BF16),
        pltpu.VMEM((2, NX - 1, 2, SUB, PHASE), BF16),
        pltpu.VMEM((2, NX - 1, 2, SUB, PHASE), BF16),
        pltpu.VMEM((2, 2, SUB, PHASE), F32),
        pltpu.VMEM((2, 2, SUB, PHASE), BF16),
        pltpu.VMEM((2, 2, 2, NZH, SUB, PHASE), BF16),
        pltpu.VMEM((2, 2, NX, SUB, PHASE), BF16),
        pltpu.VMEM((NZH, 2, NX, SUB, 128), BF16),
        pltpu.VMEM((NZH, 2, NX, SUB, 128), BF16),
        pltpu.VMEM((2, 2, 2, NY, 32, HALF), F32),
        pltpu.VMEM((2, 2, NY, 32, HALF), BF16),
        pltpu.VMEM((2, 2, NY, 32, HALF), BF16),
        pltpu.VMEM((2, NX, 2, NY, 32, 128), BF16),
        pltpu.VMEM((2, NX - 1, 2, NY, 32, 128), BF16),
        pltpu.VMEM((2, 2, NY, 32, 128), BF16),
        pltpu.VMEM((NZH, NY, 32, 128), BF16),
        pltpu.SemaphoreType.DMA((5,)),
        pltpu.SemaphoreType.DMA((COPIES,)),
        pltpu.SemaphoreType.DMA((COPIES,)),
    ]
    token_grad, weight_grad, down_grad = pl.pallas_call(
        kernel,
        out_shape=between,
        in_specs=[hbm] * 5,
        out_specs=[vmem] * 3,
        scratch_shapes=scratch,
        compiler_params=pltpu.CompilerParams(
            collective_id=0, has_side_effects=True, vmem_limit_bytes=60 * 2**20
        ),
        name="layer",
    )(tokens, cotangent, gate_weight, up_weight, down_weight)
    return pl.pallas_call(
        finish,
        out_shape=outs,
        in_specs=[hbm] * 3,
        out_specs=[hbm] * 4,
        scratch_shapes=[
            pltpu.VMEM(tokens.shape, F32),
            pltpu.VMEM((NZH, 896, 128), BF16),
            pltpu.VMEM(down_weight.shape, F32),
            pltpu.VMEM(gate_weight.shape, F32),
            pltpu.VMEM(up_weight.shape, F32),
            pltpu.SemaphoreType.DMA((NZH + 2 + 2 * NZH + 2,)),
        ],
        compiler_params=pltpu.CompilerParams(vmem_limit_bytes=60 * 2**20),
        name="finish",
    )(token_grad, weight_grad, down_grad)


def solution(mesh):
    return jax.shard_map(
        shards,
        mesh=mesh,
        in_specs=(
            P(("dep", "out"), "inp"),
            P(("dep", "out"), "inp"),
            P(("inp", "dep"), "out"),
            P(("inp", "dep"), "out"),
            P(("out", "dep"), "inp"),
        ),
        out_specs=(
            P(("dep", "out"), "inp"),
            P(("inp", "dep"), "out"),
            P(("inp", "dep"), "out"),
            P(("out", "dep"), "inp"),
        ),
        check_vma=False,
    )
```

```python
import jax
import jax.numpy as jnp
from jax import lax
from jax.experimental import pallas as pl
from jax.experimental.pallas import tpu as pltpu
from jax.sharding import PartitionSpec as P

F32, BF16 = jnp.float32, jnp.bfloat16
MESH = pl.DeviceIdType.MESH
NX, NY, NZH = 4, 4, 4
SUB = 112
HALF = 512
PHASE = 256
COPIES = 180


def nt(left_side, right_side):
    return lax.dot_general(left_side, right_side, (((1,), (1,)), ((), ())), preferred_element_type=F32)


def nn(left_side, right_side):
    return jnp.dot(left_side, right_side, preferred_element_type=F32)


def tn(left_side, right_side):
    return lax.dot_general(left_side, right_side, (((0,), (0,)), ((), ())), preferred_element_type=F32)


def local_step(gate_value, up_value, hidden_grad):
    logistic = 1.0 / (1.0 + jnp.exp(-gate_value))
    activated = gate_value * logistic
    hidden = (activated * up_value).astype(BF16)
    up_grad = (hidden_grad * activated).astype(BF16)
    gate_grad = (hidden_grad * up_value * logistic * (1.0 + gate_value * (1.0 - logistic))).astype(BF16)
    return (hidden, gate_grad, up_grad)


def lanes(block):
    return pl.ds(pl.multiple_of(block * 128, 128), 128)


def kernel(
    tok_hbm, cot_hbm, gate_hbm, up_hbm, down_hbm,
    tg_out, wg_out, down_out,
    tok_in, cot_in, gate_in, up_in, down_in,
    wt, wblk, gu, tok, cot, rs_send, rs_recv, hg_send, hg_recv, hg_own, pair,
    grads, hid, wg_send, wg_recv, part, ta_send, ta_recv, tb_send, tb_recv, tc_send, tc_recv,
    down_grad, token_grad,
    load_sems, send_sems, recv_sems,
):
    inp, y, dep = lax.axis_index("inp"), lax.axis_index("out"), lax.axis_index("dep")
    zl, x = inp // NX, inp % NX
    zh, c = dep // 2, dep % 2
    z = zh * 2 + zl

    def at(x_=x, y_=y, zh_=zh, zl_=zl, c_=c):
        return (zl_ * NX + x_, y_, zh_ * 2 + c_)

    def ring(step):
        there = (z + step + 8) % 8
        return (there // 2, there % 2)

    xs = [(x + k) % NX for k in range(NX)]
    ys = [(y + k) % NY for k in range(NY)]
    zhs = [(zh + k) % NZH for k in range(NZH)]
    cs = [c, 1 - c]
    sides = [ring(1), ring(-1)]
    around = [at(zh_=side[0], zl_=side[1]) for side in sides]
    partner = at(zl_=1 - zl)

    loads = []
    for src, dst in (
        (gate_hbm, gate_in), (up_hbm, up_in), (tok_hbm, tok_in), (cot_hbm, cot_in), (down_hbm, down_in)
    ):
        loads.append(pltpu.make_async_copy(src, dst, load_sems.at[len(loads)]))
        loads[-1].start()

    peers = [at(x_=xs[k], zh_=zhs[m]) for m in range(1, NZH) for k in range(NX)]
    peers += around
    peers += [at(y_=ys[k]) for k in range(1, NY)]
    peers += [at(x_=xs[k], c_=cs[e]) for k in range(1, NX) for e in range(2)]
    peers += [at(c_=cs[1])]
    barrier = pltpu.get_barrier_semaphore()
    for peer in peers:
        pl.semaphore_signal(barrier, inc=1, device_id=peer, device_id_type=MESH)

    for load in loads:
        load.wait()

    for q in range(NZH):
        columns = pl.ds(q * 896, 896)
        both = jnp.concatenate((gate_in[:, columns], up_in[:, columns]), axis=0)
        wt[q] = both.T.reshape(2, NX, SUB, 128)
    wblk[x * 2 + c] = wt[:, c, x]
    tok[zh // 2, zh % 2, c, y, :, lanes(x)] = tok_in[:, lanes(zh)]
    cot[zh // 2, zh % 2, c, y] = cot_in[...]

    pl.semaphore_wait(barrier, len(peers))

    started = []

    def send(src, dst, device):
        index = len(started)
        copy = pltpu.make_async_remote_copy(
            src_ref=src, dst_ref=dst, send_sem=send_sems.at[index], recv_sem=recv_sems.at[index],
            device_id=device, device_id_type=MESH,
        )
        copy.start()
        started.append(copy)
        return copy

    def arrive(copies):
        for copy in copies:
            copy.wait_recv()

    tok_first = [
        send(
            tok_in.at[:, lanes(zhs[m])],
            tok.at[zh // 2, zh % 2, c, y, :, lanes(x)],
            at(x_=xs[k], zh_=zhs[m]),
        )
        for m in (2, 1, 3, 0) for k in (2, 1, 3, 0) if (m, k) != (0, 0)
    ]
    cot_first = [send(cot_in, cot.at[zh // 2, zh % 2, c, y], at(y_=ys[k])) for k in (2, 1, 3)]

    def send_weights(q):
        return [
            send(wt.at[q, cs[e], xs[k]], wblk.at[x * 2 + c, q], at(x_=xs[k], c_=cs[e]))
            for k in (2, 1, 3, 0) for e in range(2) if (k, e) != (0, 0)
        ]

    def spread(p):
        own = tok.at[:, p, c, y]
        return {k: send(own, own, at(y_=ys[k])) for k in (2, 1, 3)}, [send(own, own, at(c_=cs[1]))]

    def share(p, by_y, by_core):
        for k in (1, 3, 2):
            by_y[k].wait_recv()
            rows = tok.at[:, p, c, ys[NY - k]]
            by_core.append(send(rows, rows, at(c_=cs[1])))
        arrive(by_core)

    order = [zhs[2], zhs[1], zhs[3], zhs[0]]
    weights = [send_weights(order[0])]
    arrive(cot_first)
    own = cot.at[zh // 2, zh % 2, c]
    cot_z = {m: send(own, own, at(zh_=zhs[m])) for m in (2, 1, 3)}
    cot_core = [send(own, own, at(c_=cs[1]))]
    arrive(tok_first)
    tok_later = [spread(p) for p in range(2)]
    for q in range(1, NZH):
        weights.append(send_weights(order[q]))

    def assemble(q):
        arrive(weights[q])
        for k in range(NX):
            even, odd = wblk[2 * k, order[q]], wblk[2 * k + 1, order[q]]
            here = pl.ds(k * 128, 128)
            gu[0, order[q], :, here] = jnp.concatenate((even[:, :64], odd[:, :64]), axis=1)
            gu[1, order[q], :, here] = jnp.concatenate((even[:, 64:], odd[:, 64:]), axis=1)

    def partial(there, p):
        rows = gu[:, there[0]].reshape(2 * SUB, HALF)
        return nt(rows, tok[there[1], p].reshape(PHASE, HALF)).reshape(2, SUB, PHASE)

    halves = [pl.ds(0, 128), pl.ds(128, 128)]

    def outset(p):
        own = partial(ring(4), p).astype(BF16)
        row = []
        for d in range(2):
            rs_send[p, d, 0, :, :, halves[d]] = own[:, :, d * 128 : (d + 1) * 128]
            row.append(
                send(rs_send.at[p, d, 0, :, :, halves[d]], rs_recv.at[p, d, 0, :, :, halves[d]], around[d])
            )
        return row

    def onward(step, p, row):
        terms = [partial(ring(4 - step), p), partial(ring(step - 4), p)]
        later = []
        for d in range(2):
            row[d].wait_recv()
            if step == 1:
                came = rs_recv[p, d, 0, :, :, halves[d]].astype(F32)
                two = [terms[d][:, :, :128], terms[d][:, :, 128:]]
                two[d] = two[d] + came
                total = jnp.concatenate(two, axis=2)
            else:
                total = terms[d] + rs_recv[p, d, step - 1].astype(F32)
            rs_send[p, d, step] = total.astype(BF16)
            later.append(send(rs_send.at[p, d, step], rs_recv.at[p, d, step], around[d]))
        return later

    def hidden_part(q, p):
        rows = down_in[pl.ds(pl.multiple_of(q * SUB, 16), SUB), :]
        return nt(rows, cot[:, p].reshape(2 * PHASE, HALF))

    def hidden_over_x(p):
        copies = []
        for k in (2, 1, 3):
            some = hidden_part(xs[k], p).astype(BF16)
            for half in range(2):
                hg_send[p, k - 1, half] = some[:, half * PHASE : (half + 1) * PHASE]
            copies.append(send(hg_send.at[p, k - 1], hg_recv.at[p, k - 1], at(x_=xs[k])))
        some = hidden_part(x, p)
        for half in range(2):
            hg_own[p, half] = some[:, half * PHASE : (half + 1) * PHASE]
        return copies

    def hidden_sum(p, half):
        total = hg_own[p, half]
        for k in range(NX - 1):
            total = total + hg_recv[p, k, half].astype(F32)
        return total

    def hidden_pair(p, by_x):
        arrive(by_x)
        pair[p, 0] = hidden_sum(p, 1 - zl).astype(BF16)
        return send(pair.at[p, 0], pair.at[p, 1], partner)

    assemble(0)
    moving, by_x, by_pair = [None, None], [None, None], [None, None]
    for p in range(2):
        share(p, *tok_later[p])
        moving[p] = outset(p)
    assemble(1)
    assemble(2)
    moving[0] = onward(1, 0, moving[0])
    for m in (1, 3, 2):
        cot_z[m].wait_recv()
        there = zhs[NZH - m]
        rows = cot.at[there // 2, there % 2, c]
        cot_core.append(send(rows, rows, at(c_=cs[1])))
    arrive(cot_core)
    by_x[0] = hidden_over_x(0)
    moving[1] = onward(1, 1, moving[1])
    by_x[1] = hidden_over_x(1)
    assemble(3)
    for p in range(2):
        moving[p] = onward(2, p, moving[p])
    by_pair[0] = hidden_pair(0, by_x[0])
    for p in range(2):
        moving[p] = onward(3, p, moving[p])
    by_pair[1] = hidden_pair(1, by_x[1])

    def chunk(there, p, step, d):
        if step == 3:
            return grads.at[there[1], p, :, there[0], :, halves[d]]
        return grads.at[there[1], p, :, there[0]]

    def forward(step, p):
        row = []
        for d in range(2):
            block = chunk(ring(-step if d == 0 else step), p, step, d)
            row.append(send(block, block, around[d]))
        return row

    for p in range(2):
        values = partial((zh, zl), p)
        hidden_grad = hidden_sum(p, zl)
        by_pair[p].wait_recv()
        hidden_grad = hidden_grad + pair[p, 1].astype(F32)
        for d in range(2):
            moving[p][d].wait_recv()
            values = values + rs_recv[p, d, 3].astype(F32)
        hidden, gate_grad, up_grad = local_step(values[0], values[1], hidden_grad)
        grads[zl, p, 0, zh] = gate_grad
        grads[zl, p, 1, zh] = up_grad
        moving[p] = forward(0, p)
        hid[zl, p, x] = hidden
        by_pair[p] = send(hid.at[zl, p, x], hid.at[zl, p, x], partner)

    returned = {}

    def weight_grads(q):
        both = jnp.zeros((2 * SUB, HALF), F32)
        for half in range(2):
            for p in range(2):
                rows = grads[half, p, :, q].reshape(2 * SUB, PHASE)
                both = both + nn(rows, tok[half, p].reshape(PHASE, HALF))
        both = both.astype(BF16)
        for k in range(NX):
            here = both[:, k * 128 : (k + 1) * 128]
            wg_send[q, 0, k] = jnp.concatenate((here[:SUB, :64], here[SUB:, :64]), axis=1)
            wg_send[q, 1, k] = jnp.concatenate((here[:SUB, 64:], here[SUB:, 64:]), axis=1)
        wg_recv[q, c, x] = wg_send[q, c, x]
        return [
            send(wg_send.at[q, cs[e], xs[k]], wg_recv.at[q, c, x], at(x_=xs[k], c_=cs[e]))
            for k in (2, 1, 3, 0) for e in range(2) if (k, e) != (0, 0)
        ]

    def over_core(p):
        for half in range(2):
            term = tn(grads[half, p].reshape(8 * SUB, PHASE), gu[...].reshape(8 * SUB, HALF))
            part[p, half] = term.reshape(2, NY, 32, HALF)
        ta_send[p] = part[p, :, cs[1]].astype(BF16)
        return send(ta_send.at[p], ta_recv.at[p], at(c_=cs[1]))

    def over_y(p, by_core):
        by_core.wait_recv()
        total = part[p, :, c] + ta_recv[p].astype(F32)
        part[p, :, c] = total
        for k in range(NY):
            tb_send[p, k] = total[:, k].astype(BF16)
        return [send(tb_send.at[p, ys[k]], tb_recv.at[p, k - 1], at(y_=ys[k])) for k in (2, 1, 3)]

    def sum_y(p, by_y):
        arrive(by_y)
        total = part[p, :, c, y]
        for k in range(NY - 1):
            total = total + tb_recv[p, k].astype(F32)
        for k in range(NX):
            tc_send[:, p, k] = total[:, :, k * 128 : (k + 1) * 128].astype(BF16)

    turn = 2 * zl - 1
    finished = [zh, (zh + turn + NZH) % NZH, (zh - turn + NZH) % NZH, zhs[2]]
    for step in range(3):
        for p in range(2):
            arrive(moving[p])
            moving[p] = forward(step + 1, p)
            if step == 0:
                by_pair[p].wait_recv()
                own = hid.at[:, p, x]
                by_x[p] = {k: send(own, own, at(x_=xs[k])) for k in (1, 3)}
            if step == 1:
                arrive(by_x[p].values())
                by_x[p] = []
                for half, k in ((0, 1), (1, 3)):
                    passed = hid.at[half, p, xs[NX - k]]
                    by_x[p].append(send(passed, passed, at(x_=xs[k])))
        returned[step] = weight_grads(finished[step])
    arrive(moving[0])
    early = over_y(0, over_core(0))
    arrive(moving[1])
    late = over_y(1, over_core(1))
    returned[3] = weight_grads(finished[3])
    sum_y(0, early)
    sum_y(1, late)
    by_place = [
        send(
            tc_send.at[zhs[m] // 2, zhs[m] % 2, xs[k]], tc_recv.at[zh, k], at(zh_=zhs[m], x_=xs[k])
        )
        for m in (2, 1, 3, 0) for k in (2, 1, 3, 0) if (m, k) != (0, 0)
    ]
    tc_recv[zh, 0] = tc_send[zh // 2, zh % 2, x]
    arrive(by_x[0])
    arrive(by_x[1])
    down = jnp.zeros((4 * SUB, HALF), F32)
    for half in range(2):
        for p in range(2):
            rows = hid[half, p].reshape(4 * SUB, PHASE)
            down = down + nn(rows, cot[half, p].reshape(PHASE, HALF))
    down_grad[...] = down
    stores = []

    def store(src, dst):
        stores.append(pltpu.make_async_copy(src, dst, load_sems.at[len(loads) + len(stores)]))
        stores[-1].start()

    store(down_grad, down_out)
    for step in range(4):
        arrive(returned[step])
        store(wg_recv.at[finished[step]], wg_out.at[finished[step]])
    arrive(by_place)
    for q in range(NZH):
        total = tc_recv[q, 0].astype(F32)
        for k in range(1, NX):
            total = total + tc_recv[q, k].astype(F32)
        token_grad[:, pl.ds(q * 128, 128)] = total
    store(token_grad, tg_out)
    for copy in started:
        copy.wait_send()
    for copy in stores:
        copy.wait()


def finish(tg_in, wg_in, down_in, tg_out, gate_out, up_out, down_out, tg, wg, down, gate, up, sems):
    loads = [pltpu.make_async_copy(wg_in.at[q], wg.at[q], sems.at[q]) for q in range(NZH)]
    loads.append(pltpu.make_async_copy(down_in, down, sems.at[NZH]))
    loads.append(pltpu.make_async_copy(tg_in, tg, sems.at[NZH + 1]))
    for load in loads:
        load.start()
    stores = []

    def store(src, dst):
        stores.append(pltpu.make_async_copy(src, dst, sems.at[len(loads) + len(stores)]))
        stores[-1].start()

    for q in range(NZH):
        loads[q].wait()
        here = pl.ds(q * 896, 896)
        block = wg[q].reshape(896, 128).T.astype(F32)
        for rows, buffer, out in ((block[:64], gate, gate_out), (block[64:], up, up_out)):
            buffer[:, here] = rows
            store(buffer.at[:, here], out.at[:, here])
        if q == 1:
            loads[NZH].wait()
            store(down, down_out)
            loads[NZH + 1].wait()
            store(tg, tg_out)
    for copy in stores:
        copy.wait()


def shards(tokens, cotangent, gate_weight, up_weight, down_weight):
    hbm = pl.BlockSpec(memory_space=pltpu.HBM)
    outs = [
        jax.ShapeDtypeStruct(tokens.shape, F32),
        jax.ShapeDtypeStruct(gate_weight.shape, F32),
        jax.ShapeDtypeStruct(up_weight.shape, F32),
        jax.ShapeDtypeStruct(down_weight.shape, F32),
    ]
    between = [
        outs[0],
        jax.ShapeDtypeStruct((NZH, 2, NX, SUB, 128), BF16),
        outs[3],
    ]
    scratch = [
        pltpu.VMEM(tokens.shape, BF16),
        pltpu.VMEM(cotangent.shape, BF16),
        pltpu.VMEM(gate_weight.shape, BF16),
        pltpu.VMEM(up_weight.shape, BF16),
        pltpu.VMEM(down_weight.shape, BF16),
        pltpu.VMEM((NZH, 2, NX, SUB, 128), BF16),
        pltpu.VMEM((2 * NX, NZH, SUB, 128), BF16),
        pltpu.VMEM((2, NZH, SUB, HALF), BF16),
        pltpu.VMEM((2, 2, 2, NY, 32, HALF), BF16),
        pltpu.VMEM((2, 2, 2, NY, 32, HALF), BF16),
        pltpu.VMEM((2, 2, 4, 2, SUB, PHASE), BF16),
        pltpu.VMEM((2, 2, 4, 2, SUB, PHASE), BF16),
        pltpu.VMEM((2, NX - 1, 2, SUB, PHASE), BF16),
        pltpu.VMEM((2, NX - 1, 2, SUB, PHASE), BF16),
        pltpu.VMEM((2, 2, SUB, PHASE), F32),
        pltpu.VMEM((2, 2, SUB, PHASE), BF16),
        pltpu.VMEM((2, 2, 2, NZH, SUB, PHASE), BF16),
        pltpu.VMEM((2, 2, NX, SUB, PHASE), BF16),
        pltpu.VMEM((NZH, 2, NX, SUB, 128), BF16),
        pltpu.VMEM((NZH, 2, NX, SUB, 128), BF16),
        pltpu.VMEM((2, 2, 2, NY, 32, HALF), F32),
        pltpu.VMEM((2, 2, NY, 32, HALF), BF16),
        pltpu.VMEM((2, 2, NY, 32, HALF), BF16),
        pltpu.VMEM((2, NY, 2, 32, HALF), BF16),
        pltpu.VMEM((2, NY - 1, 2, 32, HALF), BF16),
        pltpu.VMEM((2, 2, NX, 32, 128), BF16),
        pltpu.VMEM((NZH, NX, 32, 128), BF16),
        pltpu.VMEM(down_weight.shape, F32),
        pltpu.VMEM(tokens.shape, F32),
        pltpu.SemaphoreType.DMA((11,)),
        pltpu.SemaphoreType.DMA((COPIES,)),
        pltpu.SemaphoreType.DMA((COPIES,)),
    ]
    token_grad, weight_grad, down_grad = pl.pallas_call(
        kernel,
        out_shape=between,
        in_specs=[hbm] * 5,
        out_specs=[hbm] * 3,
        scratch_shapes=scratch,
        compiler_params=pltpu.CompilerParams(
            collective_id=0, has_side_effects=True, vmem_limit_bytes=60 * 2**20
        ),
        name="layer",
    )(tokens, cotangent, gate_weight, up_weight, down_weight)
    return pl.pallas_call(
        finish,
        out_shape=outs,
        in_specs=[hbm] * 3,
        out_specs=[hbm] * 4,
        scratch_shapes=[
            pltpu.VMEM(tokens.shape, F32),
            pltpu.VMEM((NZH, 2, NX, SUB, 128), BF16),
            pltpu.VMEM(down_weight.shape, F32),
            pltpu.VMEM(gate_weight.shape, F32),
            pltpu.VMEM(up_weight.shape, F32),
            pltpu.SemaphoreType.DMA((NZH + 2 + 2 * NZH + 2,)),
        ],
        compiler_params=pltpu.CompilerParams(vmem_limit_bytes=60 * 2**20),
        name="finish",
    )(token_grad, weight_grad, down_grad)


def solution(mesh):
    return jax.shard_map(
        shards,
        mesh=mesh,
        in_specs=(
            P(("dep", "out"), "inp"),
            P(("dep", "out"), "inp"),
            P(("inp", "dep"), "out"),
            P(("inp", "dep"), "out"),
            P(("out", "dep"), "inp"),
        ),
        out_specs=(
            P(("dep", "out"), "inp"),
            P(("inp", "dep"), "out"),
            P(("inp", "dep"), "out"),
            P(("out", "dep"), "inp"),
        ),
        check_vma=False,
    )
```

```python
import jax
import jax.numpy as jnp
from jax import lax
from jax.experimental import pallas as pl
from jax.experimental.pallas import tpu as pltpu
from jax.sharding import PartitionSpec as P

F32, BF16 = jnp.float32, jnp.bfloat16
MESH = pl.DeviceIdType.MESH
NX, NY, NZH = 4, 4, 4
SUB = 112
HALF = 512
PHASE = 256
COPIES = 190


def nt(left_side, right_side):
    return lax.dot_general(left_side, right_side, (((1,), (1,)), ((), ())), preferred_element_type=F32)


def nn(left_side, right_side):
    return jnp.dot(left_side, right_side, preferred_element_type=F32)


def tn(left_side, right_side):
    return lax.dot_general(left_side, right_side, (((0,), (0,)), ((), ())), preferred_element_type=F32)


def local_step(gate_value, up_value, hidden_grad):
    logistic = 1.0 / (1.0 + jnp.exp(-gate_value))
    activated = gate_value * logistic
    hidden = (activated * up_value).astype(BF16)
    up_grad = (hidden_grad * activated).astype(BF16)
    gate_grad = (hidden_grad * up_value * logistic * (1.0 + gate_value * (1.0 - logistic))).astype(BF16)
    return (hidden, gate_grad, up_grad)


def lanes(block):
    return pl.ds(pl.multiple_of(block * 128, 128), 128)


def kernel(
    tok_hbm, cot_hbm, gate_hbm, up_hbm, down_hbm,
    tg_out, wg_out, down_out,
    tok_in, cot_in, gate_in, up_in, down_in,
    wt, wblk, gu, tok, cot, rs_send, rs_recv, hg_send, hg_recv, hg_own, pair,
    grads, hid, wg_send, wg_recv, part, ta_send, ta_recv, tb_send, tb_recv, tc_send, tc_recv,
    down_grad, token_grad,
    load_sems, send_sems, recv_sems,
):
    inp, y, dep = lax.axis_index("inp"), lax.axis_index("out"), lax.axis_index("dep")
    zl, x = inp // NX, inp % NX
    zh, c = dep // 2, dep % 2
    z = zh * 2 + zl

    def at(x_=x, y_=y, zh_=zh, zl_=zl, c_=c):
        return (zl_ * NX + x_, y_, zh_ * 2 + c_)

    def ring(step):
        there = (z + step + 8) % 8
        return (there // 2, there % 2)

    xs = [(x + k) % NX for k in range(NX)]
    ys = [(y + k) % NY for k in range(NY)]
    zhs = [(zh + k) % NZH for k in range(NZH)]
    cs = [c, 1 - c]
    sides = [ring(1), ring(-1)]
    around = [at(zh_=side[0], zl_=side[1]) for side in sides]
    partner = at(zl_=1 - zl)

    loads = []
    for src, dst in (
        (gate_hbm, gate_in), (up_hbm, up_in), (tok_hbm, tok_in), (cot_hbm, cot_in), (down_hbm, down_in)
    ):
        loads.append(pltpu.make_async_copy(src, dst, load_sems.at[len(loads)]))
        loads[-1].start()

    peers = [at(x_=xs[k], zh_=zhs[m]) for m in range(1, NZH) for k in range(NX)]
    peers += around
    peers += [at(y_=ys[k]) for k in range(1, NY)]
    peers += [at(x_=xs[k], c_=cs[e]) for k in range(1, NX) for e in range(2)]
    peers += [at(c_=cs[1])]
    barrier = pltpu.get_barrier_semaphore()
    for peer in peers:
        pl.semaphore_signal(barrier, inc=1, device_id=peer, device_id_type=MESH)

    for load in loads:
        load.wait()

    for q in range(NZH):
        columns = pl.ds(q * 896, 896)
        both = jnp.concatenate((gate_in[:, columns], up_in[:, columns]), axis=0)
        wt[q] = both.T.reshape(2, NX, SUB, 128)
    wblk[x * 2 + c] = wt[:, c, x]
    tok[zh // 2, zh % 2, c, y, :, lanes(x)] = tok_in[:, lanes(zh)]
    cot[zh // 2, zh % 2, c, y] = cot_in[...]

    pl.semaphore_wait(barrier, len(peers))

    started = []

    def send(src, dst, device):
        index = len(started)
        copy = pltpu.make_async_remote_copy(
            src_ref=src, dst_ref=dst, send_sem=send_sems.at[index], recv_sem=recv_sems.at[index],
            device_id=device, device_id_type=MESH,
        )
        copy.start()
        started.append(copy)
        return copy

    def arrive(copies):
        for copy in copies:
            copy.wait_recv()

    tok_first = [
        send(
            tok_in.at[:, lanes(zhs[m])],
            tok.at[zh // 2, zh % 2, c, y, :, lanes(x)],
            at(x_=xs[k], zh_=zhs[m]),
        )
        for m in (2, 1, 3, 0) for k in (2, 1, 3, 0) if (m, k) != (0, 0)
    ]
    cot_first = [send(cot_in, cot.at[zh // 2, zh % 2, c, y], at(y_=ys[k])) for k in (2, 1, 3)]
    far = zhs[2]
    cot_far = send(cot_in, cot.at[zh // 2, zh % 2, c, y], at(zh_=far))

    def send_weights(q):
        return [
            send(wt.at[q, cs[e], xs[k]], wblk.at[x * 2 + c, q], at(x_=xs[k], c_=cs[e]))
            for k in (2, 1, 3, 0) for e in range(2) if (k, e) != (0, 0)
        ]

    def spread(p):
        own = tok.at[:, p, c, y]
        return {k: send(own, own, at(y_=ys[k])) for k in (2, 1, 3)}, [send(own, own, at(c_=cs[1]))]

    def share(p, by_y, by_core):
        for k in (1, 3, 2):
            by_y[k].wait_recv()
            rows = tok.at[:, p, c, ys[NY - k]]
            by_core.append(send(rows, rows, at(c_=cs[1])))
        arrive(by_core)

    order = [zhs[2], zhs[1], zhs[3], zhs[0]]
    weights = [send_weights(order[0])]
    arrive(cot_first)
    own = cot.at[zh // 2, zh % 2, c]
    cot_z = {m: send(own, own, at(zh_=zhs[m])) for m in (1, 3)}
    cot_core = [send(own, own, at(c_=cs[1]))]
    arrive(tok_first)
    tok_later = [spread(p) for p in range(2)]
    cot_far.wait_recv()
    own = cot.at[far // 2, far % 2, c, y]
    cot_y = {k: send(own, own, at(y_=ys[k])) for k in (2, 1, 3)}
    cot_core.append(send(own, own, at(c_=cs[1])))
    for q in range(1, NZH):
        weights.append(send_weights(order[q]))

    def assemble(q):
        arrive(weights[q])
        for k in range(NX):
            even, odd = wblk[2 * k, order[q]], wblk[2 * k + 1, order[q]]
            here = pl.ds(k * 128, 128)
            gu[0, order[q], :, here] = jnp.concatenate((even[:, :64], odd[:, :64]), axis=1)
            gu[1, order[q], :, here] = jnp.concatenate((even[:, 64:], odd[:, 64:]), axis=1)

    def partial(there, p):
        rows = gu[:, there[0]].reshape(2 * SUB, HALF)
        return nt(rows, tok[there[1], p].reshape(PHASE, HALF)).reshape(2, SUB, PHASE)

    halves = [pl.ds(0, 128), pl.ds(128, 128)]

    def outset(p):
        own = partial(ring(4), p).astype(BF16)
        row = []
        for d in range(2):
            rs_send[p, d, 0, :, :, halves[d]] = own[:, :, d * 128 : (d + 1) * 128]
            row.append(
                send(rs_send.at[p, d, 0, :, :, halves[d]], rs_recv.at[p, d, 0, :, :, halves[d]], around[d])
            )
        return row

    def onward(step, p, row):
        terms = [partial(ring(4 - step), p), partial(ring(step - 4), p)]
        later = []
        for d in range(2):
            row[d].wait_recv()
            if step == 1:
                came = rs_recv[p, d, 0, :, :, halves[d]].astype(F32)
                two = [terms[d][:, :, :128], terms[d][:, :, 128:]]
                two[d] = two[d] + came
                total = jnp.concatenate(two, axis=2)
            else:
                total = terms[d] + rs_recv[p, d, step - 1].astype(F32)
            rs_send[p, d, step] = total.astype(BF16)
            later.append(send(rs_send.at[p, d, step], rs_recv.at[p, d, step], around[d]))
        return later

    def hidden_part(q, p):
        rows = down_in[pl.ds(pl.multiple_of(q * SUB, 16), SUB), :]
        return nt(rows, cot[:, p].reshape(2 * PHASE, HALF))

    def hidden_over_x(p):
        copies = []
        for k in (2, 1, 3):
            some = hidden_part(xs[k], p).astype(BF16)
            for half in range(2):
                hg_send[p, k - 1, half] = some[:, half * PHASE : (half + 1) * PHASE]
            copies.append(send(hg_send.at[p, k - 1], hg_recv.at[p, k - 1], at(x_=xs[k])))
        some = hidden_part(x, p)
        for half in range(2):
            hg_own[p, half] = some[:, half * PHASE : (half + 1) * PHASE]
        return copies

    def hidden_sum(p, half):
        total = hg_own[p, half]
        for k in range(NX - 1):
            total = total + hg_recv[p, k, half].astype(F32)
        return total

    def hidden_pair(p, by_x):
        arrive(by_x)
        pair[p, 0] = hidden_sum(p, 1 - zl).astype(BF16)
        return send(pair.at[p, 0], pair.at[p, 1], partner)

    assemble(0)
    moving, by_x, by_pair = [None, None], [None, None], [None, None]
    for p in range(2):
        share(p, *tok_later[p])
        moving[p] = outset(p)
    assemble(1)
    assemble(2)
    moving[0] = onward(1, 0, moving[0])
    for m in (1, 3):
        cot_z[m].wait_recv()
        there = zhs[NZH - m]
        rows = cot.at[there // 2, there % 2, c]
        cot_core.append(send(rows, rows, at(c_=cs[1])))
    for k in (1, 3, 2):
        cot_y[k].wait_recv()
        rows = cot.at[far // 2, far % 2, c, ys[NY - k]]
        cot_core.append(send(rows, rows, at(c_=cs[1])))
    arrive(cot_core)
    by_x[0] = hidden_over_x(0)
    moving[1] = onward(1, 1, moving[1])
    by_x[1] = hidden_over_x(1)
    assemble(3)
    for p in range(2):
        moving[p] = onward(2, p, moving[p])
    by_pair[0] = hidden_pair(0, by_x[0])
    for p in range(2):
        moving[p] = onward(3, p, moving[p])
    by_pair[1] = hidden_pair(1, by_x[1])

    def chunk(there, p, step, d):
        if step == 3:
            return grads.at[there[1], p, :, there[0], :, halves[d]]
        return grads.at[there[1], p, :, there[0]]

    def forward(step, p):
        row = []
        for d in range(2):
            block = chunk(ring(-step if d == 0 else step), p, step, d)
            row.append(send(block, block, around[d]))
        return row

    for p in range(2):
        values = partial((zh, zl), p)
        hidden_grad = hidden_sum(p, zl)
        by_pair[p].wait_recv()
        hidden_grad = hidden_grad + pair[p, 1].astype(F32)
        for d in range(2):
            moving[p][d].wait_recv()
            values = values + rs_recv[p, d, 3].astype(F32)
        hidden, gate_grad, up_grad = local_step(values[0], values[1], hidden_grad)
        grads[zl, p, 0, zh] = gate_grad
        grads[zl, p, 1, zh] = up_grad
        moving[p] = forward(0, p)
        hid[zl, p, x] = hidden

    returned = {}

    def weight_grads(q):
        both = jnp.zeros((2 * SUB, HALF), F32)
        for half in range(2):
            for p in range(2):
                rows = grads[half, p, :, q].reshape(2 * SUB, PHASE)
                both = both + nn(rows, tok[half, p].reshape(PHASE, HALF))
        both = both.astype(BF16)
        for k in range(NX):
            here = both[:, k * 128 : (k + 1) * 128]
            wg_send[q, 0, k] = jnp.concatenate((here[:SUB, :64], here[SUB:, :64]), axis=1)
            wg_send[q, 1, k] = jnp.concatenate((here[:SUB, 64:], here[SUB:, 64:]), axis=1)
        wg_recv[q, c, x] = wg_send[q, c, x]
        return [
            send(wg_send.at[q, cs[e], xs[k]], wg_recv.at[q, c, x], at(x_=xs[k], c_=cs[e]))
            for k in (2, 1, 3, 0) for e in range(2) if (k, e) != (0, 0)
        ]

    def over_core(p):
        for half in range(2):
            term = tn(grads[half, p].reshape(8 * SUB, PHASE), gu[...].reshape(8 * SUB, HALF))
            part[p, half] = term.reshape(2, NY, 32, HALF)
        ta_send[p] = part[p, :, cs[1]].astype(BF16)
        return send(ta_send.at[p], ta_recv.at[p], at(c_=cs[1]))

    def over_y(p, by_core):
        by_core.wait_recv()
        total = part[p, :, c] + ta_recv[p].astype(F32)
        part[p, :, c] = total
        for k in range(NY):
            tb_send[p, k] = total[:, k].astype(BF16)
        return [send(tb_send.at[p, ys[k]], tb_recv.at[p, k - 1], at(y_=ys[k])) for k in (2, 1, 3)]

    def sum_y(p, by_y):
        arrive(by_y)
        total = part[p, :, c, y]
        for k in range(NY - 1):
            total = total + tb_recv[p, k].astype(F32)
        for k in range(NX):
            tc_send[:, p, k] = total[:, :, k * 128 : (k + 1) * 128].astype(BF16)

    turn = 2 * zl - 1
    finished = [zh, (zh + turn + NZH) % NZH, (zh - turn + NZH) % NZH, zhs[2]]
    for step in range(3):
        for p in range(2):
            arrive(moving[p])
            moving[p] = forward(step + 1, p)
        returned[step] = weight_grads(finished[step])
    by_pair = [send(hid.at[zl, p, x], hid.at[zl, p, x], partner) for p in range(2)]
    arrive(moving[0])
    by_core = over_core(0)
    for p in range(2):
        by_pair[p].wait_recv()
        own = hid.at[:, p, x]
        by_x[p] = {k: send(own, own, at(x_=xs[k])) for k in (1, 3)}
    early = over_y(0, by_core)
    arrive(moving[1])
    by_core = over_core(1)
    returned[3] = weight_grads(finished[3])
    late = over_y(1, by_core)
    for p in range(2):
        arrive(by_x[p].values())
        by_x[p] = []
        for half, k in ((0, 1), (1, 3)):
            passed = hid.at[half, p, xs[NX - k]]
            by_x[p].append(send(passed, passed, at(x_=xs[k])))
    sum_y(0, early)
    sum_y(1, late)
    by_place = [
        send(
            tc_send.at[zhs[m] // 2, zhs[m] % 2, xs[k]], tc_recv.at[zh, k], at(zh_=zhs[m], x_=xs[k])
        )
        for m in (2, 1, 3, 0) for k in (2, 1, 3, 0) if (m, k) != (0, 0)
    ]
    tc_recv[zh, 0] = tc_send[zh // 2, zh % 2, x]
    arrive(by_x[0])
    arrive(by_x[1])
    down = jnp.zeros((4 * SUB, HALF), F32)
    for half in range(2):
        for p in range(2):
            rows = hid[half, p].reshape(4 * SUB, PHASE)
            down = down + nn(rows, cot[half, p].reshape(PHASE, HALF))
    down_grad[...] = down
    stores = []

    def store(src, dst):
        stores.append(pltpu.make_async_copy(src, dst, load_sems.at[len(loads) + len(stores)]))
        stores[-1].start()

    store(down_grad, down_out)
    for step in range(4):
        arrive(returned[step])
        store(wg_recv.at[finished[step]], wg_out.at[finished[step]])
    arrive(by_place)
    for q in range(NZH):
        total = tc_recv[q, 0].astype(F32)
        for k in range(1, NX):
            total = total + tc_recv[q, k].astype(F32)
        token_grad[:, pl.ds(q * 128, 128)] = total
    store(token_grad, tg_out)
    for copy in started:
        copy.wait_send()
    for copy in stores:
        copy.wait()


def finish(tg_in, wg_in, down_in, tg_out, gate_out, up_out, down_out, tg, wg, down, gate, up, sems):
    loads = [pltpu.make_async_copy(wg_in.at[q], wg.at[q], sems.at[q]) for q in range(NZH)]
    loads.append(pltpu.make_async_copy(down_in, down, sems.at[NZH]))
    loads.append(pltpu.make_async_copy(tg_in, tg, sems.at[NZH + 1]))
    for load in loads:
        load.start()
    stores = []

    def store(src, dst):
        stores.append(pltpu.make_async_copy(src, dst, sems.at[len(loads) + len(stores)]))
        stores[-1].start()

    for q in range(NZH):
        loads[q].wait()
        here = pl.ds(q * 896, 896)
        block = wg[q].reshape(896, 128).T.astype(F32)
        for rows, buffer, out in ((block[:64], gate, gate_out), (block[64:], up, up_out)):
            buffer[:, here] = rows
            store(buffer.at[:, here], out.at[:, here])
        if q == 1:
            loads[NZH].wait()
            store(down, down_out)
            loads[NZH + 1].wait()
            store(tg, tg_out)
    for copy in stores:
        copy.wait()


def shards(tokens, cotangent, gate_weight, up_weight, down_weight):
    hbm = pl.BlockSpec(memory_space=pltpu.HBM)
    outs = [
        jax.ShapeDtypeStruct(tokens.shape, F32),
        jax.ShapeDtypeStruct(gate_weight.shape, F32),
        jax.ShapeDtypeStruct(up_weight.shape, F32),
        jax.ShapeDtypeStruct(down_weight.shape, F32),
    ]
    between = [
        outs[0],
        jax.ShapeDtypeStruct((NZH, 2, NX, SUB, 128), BF16),
        outs[3],
    ]
    scratch = [
        pltpu.VMEM(tokens.shape, BF16),
        pltpu.VMEM(cotangent.shape, BF16),
        pltpu.VMEM(gate_weight.shape, BF16),
        pltpu.VMEM(up_weight.shape, BF16),
        pltpu.VMEM(down_weight.shape, BF16),
        pltpu.VMEM((NZH, 2, NX, SUB, 128), BF16),
        pltpu.VMEM((2 * NX, NZH, SUB, 128), BF16),
        pltpu.VMEM((2, NZH, SUB, HALF), BF16),
        pltpu.VMEM((2, 2, 2, NY, 32, HALF), BF16),
        pltpu.VMEM((2, 2, 2, NY, 32, HALF), BF16),
        pltpu.VMEM((2, 2, 4, 2, SUB, PHASE), BF16),
        pltpu.VMEM((2, 2, 4, 2, SUB, PHASE), BF16),
        pltpu.VMEM((2, NX - 1, 2, SUB, PHASE), BF16),
        pltpu.VMEM((2, NX - 1, 2, SUB, PHASE), BF16),
        pltpu.VMEM((2, 2, SUB, PHASE), F32),
        pltpu.VMEM((2, 2, SUB, PHASE), BF16),
        pltpu.VMEM((2, 2, 2, NZH, SUB, PHASE), BF16),
        pltpu.VMEM((2, 2, NX, SUB, PHASE), BF16),
        pltpu.VMEM((NZH, 2, NX, SUB, 128), BF16),
        pltpu.VMEM((NZH, 2, NX, SUB, 128), BF16),
        pltpu.VMEM((2, 2, 2, NY, 32, HALF), F32),
        pltpu.VMEM((2, 2, NY, 32, HALF), BF16),
        pltpu.VMEM((2, 2, NY, 32, HALF), BF16),
        pltpu.VMEM((2, NY, 2, 32, HALF), BF16),
        pltpu.VMEM((2, NY - 1, 2, 32, HALF), BF16),
        pltpu.VMEM((2, 2, NX, 32, 128), BF16),
        pltpu.VMEM((NZH, NX, 32, 128), BF16),
        pltpu.VMEM(down_weight.shape, F32),
        pltpu.VMEM(tokens.shape, F32),
        pltpu.SemaphoreType.DMA((11,)),
        pltpu.SemaphoreType.DMA((COPIES,)),
        pltpu.SemaphoreType.DMA((COPIES,)),
    ]
    token_grad, weight_grad, down_grad = pl.pallas_call(
        kernel,
        out_shape=between,
        in_specs=[hbm] * 5,
        out_specs=[hbm] * 3,
        scratch_shapes=scratch,
        compiler_params=pltpu.CompilerParams(
            collective_id=0, has_side_effects=True, vmem_limit_bytes=60 * 2**20
        ),
        name="layer",
    )(tokens, cotangent, gate_weight, up_weight, down_weight)
    return pl.pallas_call(
        finish,
        out_shape=outs,
        in_specs=[hbm] * 3,
        out_specs=[hbm] * 4,
        scratch_shapes=[
            pltpu.VMEM(tokens.shape, F32),
            pltpu.VMEM((NZH, 2, NX, SUB, 128), BF16),
            pltpu.VMEM(down_weight.shape, F32),
            pltpu.VMEM(gate_weight.shape, F32),
            pltpu.VMEM(up_weight.shape, F32),
            pltpu.SemaphoreType.DMA((NZH + 2 + 2 * NZH + 2,)),
        ],
        compiler_params=pltpu.CompilerParams(vmem_limit_bytes=60 * 2**20),
        name="finish",
    )(token_grad, weight_grad, down_grad)


def solution(mesh):
    return jax.shard_map(
        shards,
        mesh=mesh,
        in_specs=(
            P(("dep", "out"), "inp"),
            P(("dep", "out"), "inp"),
            P(("inp", "dep"), "out"),
            P(("inp", "dep"), "out"),
            P(("out", "dep"), "inp"),
        ),
        out_specs=(
            P(("dep", "out"), "inp"),
            P(("inp", "dep"), "out"),
            P(("inp", "dep"), "out"),
            P(("out", "dep"), "inp"),
        ),
        check_vma=False,
    )
```

```python
import jax
import jax.numpy as jnp
from jax import lax
from jax.experimental import pallas as pl
from jax.experimental.pallas import tpu as pltpu
from jax.sharding import PartitionSpec as P

F32, BF16 = jnp.float32, jnp.bfloat16
MESH = pl.DeviceIdType.MESH
NX, NY, NZH = 4, 4, 4
SUB = 112
HALF = 512
PHASE = 256
COPIES = 200


def nt(left_side, right_side):
    return lax.dot_general(left_side, right_side, (((1,), (1,)), ((), ())), preferred_element_type=F32)


def nn(left_side, right_side):
    return jnp.dot(left_side, right_side, preferred_element_type=F32)


def tn(left_side, right_side):
    return lax.dot_general(left_side, right_side, (((0,), (0,)), ((), ())), preferred_element_type=F32)


def local_step(gate_value, up_value, hidden_grad):
    logistic = 1.0 / (1.0 + jnp.exp(-gate_value))
    activated = gate_value * logistic
    hidden = (activated * up_value).astype(BF16)
    up_grad = (hidden_grad * activated).astype(BF16)
    gate_grad = (hidden_grad * up_value * logistic * (1.0 + gate_value * (1.0 - logistic))).astype(BF16)
    return (hidden, gate_grad, up_grad)


def lanes(block):
    return pl.ds(pl.multiple_of(block * 128, 128), 128)


def kernel(
    tok_hbm, cot_hbm, gate_hbm, up_hbm, down_hbm,
    tg_out, wg_out, down_out,
    tok_in, cot_in, gate_in, up_in, down_in,
    wt, wblk, gu, tok, cot, rs_send, rs_recv, hg_send, hg_recv, pair,
    grads, hid, wg_send, wg_recv, part, ta_send, ta_recv, tb_send, tb_recv, tc_send, tc_recv,
    down_grad, token_grad,
    load_sems, send_sems, recv_sems,
):
    inp, y, dep = lax.axis_index("inp"), lax.axis_index("out"), lax.axis_index("dep")
    zl, x = inp // NX, inp % NX
    zh, c = dep // 2, dep % 2
    z = zh * 2 + zl

    def at(x_=x, y_=y, zh_=zh, zl_=zl, c_=c):
        return (zl_ * NX + x_, y_, zh_ * 2 + c_)

    def ring(step):
        there = (z + step + 8) % 8
        return (there // 2, there % 2)

    xs = [(x + k) % NX for k in range(NX)]
    ys = [(y + k) % NY for k in range(NY)]
    zhs = [(zh + k) % NZH for k in range(NZH)]
    cs = [c, 1 - c]
    sides = [ring(1), ring(-1)]
    around = [at(zh_=side[0], zl_=side[1]) for side in sides]
    partner = at(zl_=1 - zl)

    loads = []
    for src, dst in (
        (gate_hbm, gate_in), (up_hbm, up_in), (tok_hbm, tok_in), (cot_hbm, cot_in), (down_hbm, down_in)
    ):
        loads.append(pltpu.make_async_copy(src, dst, load_sems.at[len(loads)]))
        loads[-1].start()

    peers = [at(x_=xs[k], zh_=zhs[m]) for m in range(1, NZH) for k in range(NX)]
    peers += around
    peers += [at(y_=ys[k]) for k in range(1, NY)]
    peers += [at(x_=xs[k], c_=cs[e]) for k in range(1, NX) for e in range(2)]
    peers += [at(c_=cs[1])]
    barrier = pltpu.get_barrier_semaphore()
    for peer in peers:
        pl.semaphore_signal(barrier, inc=1, device_id=peer, device_id_type=MESH)

    for load in loads:
        load.wait()

    for q in range(NZH):
        columns = pl.ds(q * 896, 896)
        both = jnp.concatenate((gate_in[:, columns], up_in[:, columns]), axis=0)
        wt[q] = both.T.reshape(2, NX, SUB, 128)
    wblk[x * 2 + c] = wt[:, c, x]
    tok[zh // 2, zh % 2, c, y, :, lanes(x)] = tok_in[:, lanes(zh)]
    cot[zh // 2, zh % 2, c, y] = cot_in[...]

    pl.semaphore_wait(barrier, len(peers))

    started = []

    def send(src, dst, device):
        index = len(started)
        copy = pltpu.make_async_remote_copy(
            src_ref=src, dst_ref=dst, send_sem=send_sems.at[index], recv_sem=recv_sems.at[index],
            device_id=device, device_id_type=MESH,
        )
        copy.start()
        started.append(copy)
        return copy

    def arrive(copies):
        for copy in copies:
            copy.wait_recv()

    tok_first = [
        send(
            tok_in.at[:, lanes(zhs[m])],
            tok.at[zh // 2, zh % 2, c, y, :, lanes(x)],
            at(x_=xs[k], zh_=zhs[m]),
        )
        for m in (2, 1, 3, 0) for k in (2, 1, 3, 0) if (m, k) != (0, 0)
    ]
    cot_first = [send(cot_in, cot.at[zh // 2, zh % 2, c, y], at(y_=ys[k])) for k in (2, 1, 3)]
    far = zhs[2]
    cot_far = send(cot_in, cot.at[zh // 2, zh % 2, c, y], at(zh_=far))

    def send_weights(q):
        return [
            send(wt.at[q, cs[e], xs[k]], wblk.at[x * 2 + c, q], at(x_=xs[k], c_=cs[e]))
            for k in (2, 1, 3, 0) for e in range(2) if (k, e) != (0, 0)
        ]

    def spread(p):
        own = tok.at[:, p, c, y]
        return {k: send(own, own, at(y_=ys[k])) for k in (2, 1, 3)}, [send(own, own, at(c_=cs[1]))]

    def share(p, by_y, by_core):
        for k in (1, 3, 2):
            by_y[k].wait_recv()
            rows = tok.at[:, p, c, ys[NY - k]]
            by_core.append(send(rows, rows, at(c_=cs[1])))
        arrive(by_core)

    order = [zhs[2], zhs[1], zhs[3], zhs[0]]
    weights = [send_weights(order[0])]
    arrive(cot_first)
    own = cot.at[zh // 2, zh % 2, c]
    cot_z = {m: send(own, own, at(zh_=zhs[m])) for m in (1, 3)}
    cot_core = [send(own, own, at(c_=cs[1]))]
    arrive(tok_first)
    tok_later = [spread(p) for p in range(2)]
    cot_far.wait_recv()
    own = cot.at[far // 2, far % 2, c, y]
    cot_y = {k: send(own, own, at(y_=ys[k])) for k in (2, 1, 3)}
    cot_core.append(send(own, own, at(c_=cs[1])))
    for q in range(1, NZH):
        weights.append(send_weights(order[q]))

    def assemble(q):
        arrive(weights[q])
        for k in range(NX):
            even, odd = wblk[2 * k, order[q]], wblk[2 * k + 1, order[q]]
            here = pl.ds(k * 128, 128)
            gu[0, order[q], :, here] = jnp.concatenate((even[:, :64], odd[:, :64]), axis=1)
            gu[1, order[q], :, here] = jnp.concatenate((even[:, 64:], odd[:, 64:]), axis=1)

    def partial(there, p):
        rows = gu[:, there[0]].reshape(2 * SUB, HALF)
        return nt(rows, tok[there[1], p].reshape(PHASE, HALF)).reshape(2, SUB, PHASE)

    halves = [pl.ds(0, 128), pl.ds(128, 128)]

    def outset(p):
        own = partial(ring(4), p).astype(BF16)
        row = []
        for d in range(2):
            rs_send[p, d, 0, :, :, halves[d]] = own[:, :, d * 128 : (d + 1) * 128]
            row.append(
                send(rs_send.at[p, d, 0, :, :, halves[d]], rs_recv.at[p, d, 0, :, :, halves[d]], around[d])
            )
        return row

    def onward(step, p, row):
        there = [ring(4 - step), ring(step - 4)]
        rows = [gu[:, one[0]].reshape(2 * SUB, HALF) for one in there]
        both = nt(jnp.concatenate(rows, axis=0), tok[there[0][1], p].reshape(PHASE, HALF))
        terms = both.reshape(2, 2, SUB, PHASE)
        later = []
        for d in range(2):
            row[d].wait_recv()
            if step == 1:
                came = rs_recv[p, d, 0, :, :, halves[d]].astype(F32)
                two = [terms[d][:, :, :128], terms[d][:, :, 128:]]
                two[d] = two[d] + came
                total = jnp.concatenate(two, axis=2)
            else:
                total = terms[d] + rs_recv[p, d, step - 1].astype(F32)
            rs_send[p, d, step] = total.astype(BF16)
            later.append(send(rs_send.at[p, d, step], rs_recv.at[p, d, step], around[d]))
        return later

    def hidden_over_x(p):
        full = nt(down_in[...], cot[:, p].reshape(2 * PHASE, HALF)).astype(BF16)
        for half in range(2):
            some = full[:, half * PHASE : (half + 1) * PHASE]
            hg_send[p, :, half] = some.reshape(NX, SUB, PHASE)
        return [send(hg_send.at[p, xs[k]], hg_recv.at[p, k - 1], at(x_=xs[k])) for k in (2, 1, 3)]

    def hidden_sum(p, half):
        total = hg_send[p, x, half].astype(F32)
        for k in range(NX - 1):
            total = total + hg_recv[p, k, half].astype(F32)
        return total

    def hidden_pair(p, by_x):
        arrive(by_x)
        pair[p, 0] = hidden_sum(p, 1 - zl).astype(BF16)
        return send(pair.at[p, 0], pair.at[p, 1], partner)

    assemble(0)
    moving, by_x, by_pair = [None, None], [None, None], [None, None]
    for p in range(2):
        share(p, *tok_later[p])
        moving[p] = outset(p)
    assemble(1)
    assemble(2)
    moving[0] = onward(1, 0, moving[0])
    for m in (1, 3):
        cot_z[m].wait_recv()
        there = zhs[NZH - m]
        rows = cot.at[there // 2, there % 2, c]
        cot_core.append(send(rows, rows, at(c_=cs[1])))
    for k in (1, 3, 2):
        cot_y[k].wait_recv()
        rows = cot.at[far // 2, far % 2, c, ys[NY - k]]
        cot_core.append(send(rows, rows, at(c_=cs[1])))
    arrive(cot_core)
    by_x[0] = hidden_over_x(0)
    moving[1] = onward(1, 1, moving[1])
    by_x[1] = hidden_over_x(1)
    assemble(3)
    for p in range(2):
        moving[p] = onward(2, p, moving[p])
    by_pair[0] = hidden_pair(0, by_x[0])
    for p in range(2):
        moving[p] = onward(3, p, moving[p])
    by_pair[1] = hidden_pair(1, by_x[1])

    def chunk(there, p, step, d):
        if step == 3:
            return grads.at[there[1], p, :, there[0], :, halves[d]]
        return grads.at[there[1], p, :, there[0]]

    def forward(step, p):
        row = []
        for d in range(2):
            block = chunk(ring(-step if d == 0 else step), p, step, d)
            row.append(send(block, block, around[d]))
        return row

    for p in range(2):
        values = partial((zh, zl), p)
        hidden_grad = hidden_sum(p, zl)
        by_pair[p].wait_recv()
        hidden_grad = hidden_grad + pair[p, 1].astype(F32)
        for d in range(2):
            moving[p][d].wait_recv()
            values = values + rs_recv[p, d, 3].astype(F32)
        hidden, gate_grad, up_grad = local_step(values[0], values[1], hidden_grad)
        grads[zl, p, 0, zh] = gate_grad
        grads[zl, p, 1, zh] = up_grad
        moving[p] = forward(0, p)
        hid[zl, p, x] = hidden

    returned = {}

    def weight_grads(q):
        both = jnp.zeros((2 * SUB, HALF), F32)
        for half in range(2):
            for p in range(2):
                rows = grads[half, p, :, q].reshape(2 * SUB, PHASE)
                both = both + nn(rows, tok[half, p].reshape(PHASE, HALF))
        both = both.astype(BF16)
        for k in range(NX):
            here = both[:, k * 128 : (k + 1) * 128]
            wg_send[q, 0, k] = jnp.concatenate((here[:SUB, :64], here[SUB:, :64]), axis=1)
            wg_send[q, 1, k] = jnp.concatenate((here[:SUB, 64:], here[SUB:, 64:]), axis=1)
        wg_recv[q, c, x] = wg_send[q, c, x]
        return [
            send(wg_send.at[q, cs[e], xs[k]], wg_recv.at[q, c, x], at(x_=xs[k], c_=cs[e]))
            for k in (2, 1, 3, 0) for e in range(2) if (k, e) != (0, 0)
        ]

    def over_core(half, p):
        term = tn(grads[half, p].reshape(8 * SUB, PHASE), gu[...].reshape(8 * SUB, HALF))
        part[half, p] = term.reshape(2, NY, 32, HALF)
        ta_send[half, p] = part[half, p, cs[1]].astype(BF16)
        return send(ta_send.at[half, p], ta_recv.at[half, p], at(c_=cs[1]))

    def over_y(half, p, by_core):
        by_core.wait_recv()
        total = part[half, p, c] + ta_recv[half, p].astype(F32)
        part[half, p, c] = total
        tb_send[half, p] = total.astype(BF16)
        return [
            send(tb_send.at[half, p, ys[k]], tb_recv.at[half, p, k - 1], at(y_=ys[k])) for k in (2, 1, 3)
        ]

    def sum_y(half, p, by_y):
        arrive(by_y)
        total = part[half, p, c, y]
        for k in range(NY - 1):
            total = total + tb_recv[half, p, k].astype(F32)
        for k in range(NX):
            tc_send[half, p, k] = total[:, k * 128 : (k + 1) * 128].astype(BF16)

    turn = 2 * zl - 1
    finished = [zh, (zh + turn + NZH) % NZH, (zh - turn + NZH) % NZH, zhs[2]]
    for step in range(3):
        for p in range(2):
            arrive(moving[p])
            moving[p] = forward(step + 1, p)
        returned[step] = weight_grads(finished[step])
    by_pair = [send(hid.at[zl, p, x], hid.at[zl, p, x], partner) for p in range(2)]
    early = [over_core(1 - zl, p) for p in range(2)]
    early = [over_y(1 - zl, p, early[p]) for p in range(2)]
    arrive(moving[0])
    by_core = over_core(zl, 0)
    for p in range(2):
        by_pair[p].wait_recv()
        own = hid.at[:, p, x]
        by_x[p] = {k: send(own, own, at(x_=xs[k])) for k in (1, 3)}
    late = [over_y(zl, 0, by_core)]
    arrive(moving[1])
    by_core = over_core(zl, 1)
    returned[3] = weight_grads(finished[3])
    late.append(over_y(zl, 1, by_core))
    for p in range(2):
        arrive(by_x[p].values())
        by_x[p] = []
        for half, k in ((0, 1), (1, 3)):
            passed = hid.at[half, p, xs[NX - k]]
            by_x[p].append(send(passed, passed, at(x_=xs[k])))
    for p in range(2):
        sum_y(1 - zl, p, early[p])
    for p in range(2):
        sum_y(zl, p, late[p])
    by_place = [
        send(
            tc_send.at[zhs[m] // 2, zhs[m] % 2, xs[k]], tc_recv.at[zh, k], at(zh_=zhs[m], x_=xs[k])
        )
        for m in (2, 1, 3, 0) for k in (2, 1, 3, 0) if (m, k) != (0, 0)
    ]
    tc_recv[zh, 0] = tc_send[zh // 2, zh % 2, x]
    arrive(by_x[0])
    arrive(by_x[1])
    down = jnp.zeros((4 * SUB, HALF), F32)
    for half in range(2):
        for p in range(2):
            rows = hid[half, p].reshape(4 * SUB, PHASE)
            down = down + nn(rows, cot[half, p].reshape(PHASE, HALF))
    down_grad[...] = down
    stores = []

    def store(src, dst):
        stores.append(pltpu.make_async_copy(src, dst, load_sems.at[len(loads) + len(stores)]))
        stores[-1].start()

    store(down_grad, down_out)
    for step in range(4):
        arrive(returned[step])
        store(wg_recv.at[finished[step]], wg_out.at[finished[step]])
    arrive(by_place)
    for q in range(NZH):
        total = tc_recv[q, 0].astype(F32)
        for k in range(1, NX):
            total = total + tc_recv[q, k].astype(F32)
        token_grad[:, pl.ds(q * 128, 128)] = total
    store(token_grad, tg_out)
    for copy in started:
        copy.wait_send()
    for copy in stores:
        copy.wait()


def finish(tg_in, wg_in, down_in, tg_out, gate_out, up_out, down_out, tg, wg, down, gate, up, sems):
    loads = [pltpu.make_async_copy(wg_in.at[q], wg.at[q], sems.at[q]) for q in range(NZH)]
    loads.append(pltpu.make_async_copy(down_in, down, sems.at[NZH]))
    loads.append(pltpu.make_async_copy(tg_in, tg, sems.at[NZH + 1]))
    for load in loads:
        load.start()
    stores = []

    def store(src, dst):
        stores.append(pltpu.make_async_copy(src, dst, sems.at[len(loads) + len(stores)]))
        stores[-1].start()

    for q in range(NZH):
        loads[q].wait()
        here = pl.ds(q * 896, 896)
        block = wg[q].reshape(896, 128).T.astype(F32)
        for rows, buffer, out in ((block[:64], gate, gate_out), (block[64:], up, up_out)):
            buffer[:, here] = rows
            store(buffer.at[:, here], out.at[:, here])
        if q == 1:
            loads[NZH].wait()
            store(down, down_out)
            loads[NZH + 1].wait()
            store(tg, tg_out)
    for copy in stores:
        copy.wait()


def shards(tokens, cotangent, gate_weight, up_weight, down_weight):
    hbm = pl.BlockSpec(memory_space=pltpu.HBM)
    outs = [
        jax.ShapeDtypeStruct(tokens.shape, F32),
        jax.ShapeDtypeStruct(gate_weight.shape, F32),
        jax.ShapeDtypeStruct(up_weight.shape, F32),
        jax.ShapeDtypeStruct(down_weight.shape, F32),
    ]
    between = [
        outs[0],
        jax.ShapeDtypeStruct((NZH, 2, NX, SUB, 128), BF16),
        outs[3],
    ]
    scratch = [
        pltpu.VMEM(tokens.shape, BF16),
        pltpu.VMEM(cotangent.shape, BF16),
        pltpu.VMEM(gate_weight.shape, BF16),
        pltpu.VMEM(up_weight.shape, BF16),
        pltpu.VMEM(down_weight.shape, BF16),
        pltpu.VMEM((NZH, 2, NX, SUB, 128), BF16),
        pltpu.VMEM((2 * NX, NZH, SUB, 128), BF16),
        pltpu.VMEM((2, NZH, SUB, HALF), BF16),
        pltpu.VMEM((2, 2, 2, NY, 32, HALF), BF16),
        pltpu.VMEM((2, 2, 2, NY, 32, HALF), BF16),
        pltpu.VMEM((2, 2, 4, 2, SUB, PHASE), BF16),
        pltpu.VMEM((2, 2, 4, 2, SUB, PHASE), BF16),
        pltpu.VMEM((2, NX, 2, SUB, PHASE), BF16),
        pltpu.VMEM((2, NX - 1, 2, SUB, PHASE), BF16),
        pltpu.VMEM((2, 2, SUB, PHASE), BF16),
        pltpu.VMEM((2, 2, 2, NZH, SUB, PHASE), BF16),
        pltpu.VMEM((2, 2, NX, SUB, PHASE), BF16),
        pltpu.VMEM((NZH, 2, NX, SUB, 128), BF16),
        pltpu.VMEM((NZH, 2, NX, SUB, 128), BF16),
        pltpu.VMEM((2, 2, 2, NY, 32, HALF), F32),
        pltpu.VMEM((2, 2, NY, 32, HALF), BF16),
        pltpu.VMEM((2, 2, NY, 32, HALF), BF16),
        pltpu.VMEM((2, 2, NY, 32, HALF), BF16),
        pltpu.VMEM((2, 2, NY - 1, 32, HALF), BF16),
        pltpu.VMEM((2, 2, NX, 32, 128), BF16),
        pltpu.VMEM((NZH, NX, 32, 128), BF16),
        pltpu.VMEM(down_weight.shape, F32),
        pltpu.VMEM(tokens.shape, F32),
        pltpu.SemaphoreType.DMA((11,)),
        pltpu.SemaphoreType.DMA((COPIES,)),
        pltpu.SemaphoreType.DMA((COPIES,)),
    ]
    token_grad, weight_grad, down_grad = pl.pallas_call(
        kernel,
        out_shape=between,
        in_specs=[hbm] * 5,
        out_specs=[hbm] * 3,
        scratch_shapes=scratch,
        compiler_params=pltpu.CompilerParams(
            collective_id=0, has_side_effects=True, vmem_limit_bytes=60 * 2**20
        ),
        name="layer",
    )(tokens, cotangent, gate_weight, up_weight, down_weight)
    return pl.pallas_call(
        finish,
        out_shape=outs,
        in_specs=[hbm] * 3,
        out_specs=[hbm] * 4,
        scratch_shapes=[
            pltpu.VMEM(tokens.shape, F32),
            pltpu.VMEM((NZH, 2, NX, SUB, 128), BF16),
            pltpu.VMEM(down_weight.shape, F32),
            pltpu.VMEM(gate_weight.shape, F32),
            pltpu.VMEM(up_weight.shape, F32),
            pltpu.SemaphoreType.DMA((NZH + 2 + 2 * NZH + 2,)),
        ],
        compiler_params=pltpu.CompilerParams(vmem_limit_bytes=60 * 2**20),
        name="finish",
    )(token_grad, weight_grad, down_grad)


def solution(mesh):
    return jax.shard_map(
        shards,
        mesh=mesh,
        in_specs=(
            P(("dep", "out"), "inp"),
            P(("dep", "out"), "inp"),
            P(("inp", "dep"), "out"),
            P(("inp", "dep"), "out"),
            P(("out", "dep"), "inp"),
        ),
        out_specs=(
            P(("dep", "out"), "inp"),
            P(("inp", "dep"), "out"),
            P(("inp", "dep"), "out"),
            P(("out", "dep"), "inp"),
        ),
        check_vma=False,
    )
```

```python
import jax
import jax.numpy as jnp
from jax import lax
from jax.experimental import pallas as pl
from jax.experimental.pallas import tpu as pltpu
from jax.sharding import PartitionSpec as P

F32, BF16 = jnp.float32, jnp.bfloat16
MESH = pl.DeviceIdType.MESH
NX, NY, NZH = 4, 4, 4
SUB = 112
HALF = 512
PHASE = 256
COPIES = 190


def nt(left_side, right_side):
    return lax.dot_general(left_side, right_side, (((1,), (1,)), ((), ())), preferred_element_type=F32)


def nn(left_side, right_side):
    return jnp.dot(left_side, right_side, preferred_element_type=F32)


def tn(left_side, right_side):
    return lax.dot_general(left_side, right_side, (((0,), (0,)), ((), ())), preferred_element_type=F32)


def local_step(gate_value, up_value, hidden_grad):
    logistic = 1.0 / (1.0 + jnp.exp(-gate_value))
    activated = gate_value * logistic
    hidden = (activated * up_value).astype(BF16)
    up_grad = (hidden_grad * activated).astype(BF16)
    gate_grad = (hidden_grad * up_value * logistic * (1.0 + gate_value * (1.0 - logistic))).astype(BF16)
    return (hidden, gate_grad, up_grad)


def lanes(block):
    return pl.ds(pl.multiple_of(block * 128, 128), 128)


def kernel(
    tok_hbm, cot_hbm, gate_hbm, up_hbm, down_hbm,
    tg_out, wg_out, down_out,
    tok_in, cot_in, gate_in, up_in, down_in,
    wt, wblk, gu, tok, cot, rs_send, rs_recv, hg_send, hg_recv, pair,
    grads, hid, wg_send, wg_recv, part, ta_send, ta_recv, tb_send, tb_recv, tc_send, tc_recv,
    down_grad, token_grad,
    load_sems, send_sems, recv_sems,
):
    inp, y, dep = lax.axis_index("inp"), lax.axis_index("out"), lax.axis_index("dep")
    zl, x = inp // NX, inp % NX
    zh, c = dep // 2, dep % 2
    z = zh * 2 + zl

    def at(x_=x, y_=y, zh_=zh, zl_=zl, c_=c):
        return (zl_ * NX + x_, y_, zh_ * 2 + c_)

    def ring(step):
        there = (z + step + 8) % 8
        return (there // 2, there % 2)

    xs = [(x + k) % NX for k in range(NX)]
    ys = [(y + k) % NY for k in range(NY)]
    zhs = [(zh + k) % NZH for k in range(NZH)]
    cs = [c, 1 - c]
    sides = [ring(1), ring(-1)]
    around = [at(zh_=side[0], zl_=side[1]) for side in sides]
    partner = at(zl_=1 - zl)

    loads = []
    for src, dst in (
        (gate_hbm, gate_in), (up_hbm, up_in), (tok_hbm, tok_in), (cot_hbm, cot_in), (down_hbm, down_in)
    ):
        loads.append(pltpu.make_async_copy(src, dst, load_sems.at[len(loads)]))
        loads[-1].start()

    peers = [at(x_=xs[k], zh_=zhs[m]) for m in range(1, NZH) for k in range(NX)]
    peers += around
    peers += [at(y_=ys[k]) for k in range(1, NY)]
    peers += [at(x_=xs[k], c_=cs[e]) for k in range(1, NX) for e in range(2)]
    peers += [at(c_=cs[1])]
    barrier = pltpu.get_barrier_semaphore()
    for peer in peers:
        pl.semaphore_signal(barrier, inc=1, device_id=peer, device_id_type=MESH)

    for load in loads:
        load.wait()

    for q in range(NZH):
        columns = pl.ds(q * 896, 896)
        both = jnp.concatenate((gate_in[:, columns], up_in[:, columns]), axis=0)
        wt[q] = both.T.reshape(2, NX, SUB, 128)
    wblk[x * 2 + c] = wt[:, c, x]
    tok[zh // 2, zh % 2, c, y, :, lanes(x)] = tok_in[:, lanes(zh)]
    cot[zh // 2, zh % 2, c, y] = cot_in[...]

    pl.semaphore_wait(barrier, len(peers))

    started = []

    def send(src, dst, device):
        index = len(started)
        copy = pltpu.make_async_remote_copy(
            src_ref=src, dst_ref=dst, send_sem=send_sems.at[index], recv_sem=recv_sems.at[index],
            device_id=device, device_id_type=MESH,
        )
        copy.start()
        started.append(copy)
        return copy

    def arrive(copies):
        for copy in copies:
            copy.wait_recv()

    tok_first = [
        send(
            tok_in.at[:, lanes(zhs[m])],
            tok.at[zh // 2, zh % 2, c, y, :, lanes(x)],
            at(x_=xs[k], zh_=zhs[m]),
        )
        for m in (2, 1, 3, 0) for k in (2, 1, 3, 0) if (m, k) != (0, 0)
    ]
    cot_first = [send(cot_in, cot.at[zh // 2, zh % 2, c, y], at(y_=ys[k])) for k in (2, 1, 3)]
    far = zhs[2]
    cot_far = send(cot_in, cot.at[zh // 2, zh % 2, c, y], at(zh_=far))

    def send_weights(q):
        return [
            send(wt.at[q, cs[e], xs[k]], wblk.at[x * 2 + c, q], at(x_=xs[k], c_=cs[e]))
            for k in (2, 1, 3, 0) for e in range(2) if (k, e) != (0, 0)
        ]

    def spread(p):
        own = tok.at[:, p, c, y]
        return {k: send(own, own, at(y_=ys[k])) for k in (2, 1, 3)}, [send(own, own, at(c_=cs[1]))]

    def share(p, by_y, by_core):
        for k in (1, 3, 2):
            by_y[k].wait_recv()
            rows = tok.at[:, p, c, ys[NY - k]]
            by_core.append(send(rows, rows, at(c_=cs[1])))
        arrive(by_core)

    order = [zhs[2], zhs[1], zhs[3], zhs[0]]
    weights = [send_weights(order[0])]
    arrive(cot_first)
    own = cot.at[zh // 2, zh % 2, c]
    cot_z = {m: send(own, own, at(zh_=zhs[m])) for m in (1, 3)}
    cot_core = [send(own, own, at(c_=cs[1]))]
    arrive(tok_first)
    tok_later = [spread(p) for p in range(2)]
    for q in range(1, NZH):
        weights.append(send_weights(order[q]))
    cot_far.wait_recv()
    own = cot.at[far // 2, far % 2, c, y]
    cot_y = {k: send(own, own, at(y_=ys[k])) for k in (2, 1, 3)}
    cot_core.append(send(own, own, at(c_=cs[1])))

    def assemble(q):
        arrive(weights[q])
        for k in range(NX):
            even, odd = wblk[2 * k, order[q]], wblk[2 * k + 1, order[q]]
            here = pl.ds(k * 128, 128)
            gu[0, order[q], :, here] = jnp.concatenate((even[:, :64], odd[:, :64]), axis=1)
            gu[1, order[q], :, here] = jnp.concatenate((even[:, 64:], odd[:, 64:]), axis=1)

    def partial(there, p):
        rows = gu[:, there[0]].reshape(2 * SUB, HALF)
        return nt(rows, tok[there[1], p].reshape(PHASE, HALF)).reshape(2, SUB, PHASE)

    halves = [pl.ds(0, 128), pl.ds(128, 128)]

    def outset(p):
        own = partial(ring(4), p).astype(BF16)
        row = []
        for d in range(2):
            rs_send[p, d, 0, :, :, halves[d]] = own[:, :, d * 128 : (d + 1) * 128]
            row.append(
                send(rs_send.at[p, d, 0, :, :, halves[d]], rs_recv.at[p, d, 0, :, :, halves[d]], around[d])
            )
        return row

    def onward(step, p, row):
        there = [ring(4 - step), ring(step - 4)]
        rows = [gu[:, one[0]].reshape(2 * SUB, HALF) for one in there]
        both = nt(jnp.concatenate(rows, axis=0), tok[there[0][1], p].reshape(PHASE, HALF))
        terms = both.reshape(2, 2, SUB, PHASE)
        later = []
        for d in range(2):
            row[d].wait_recv()
            if step == 1:
                came = rs_recv[p, d, 0, :, :, halves[d]].astype(F32)
                two = [terms[d][:, :, :128], terms[d][:, :, 128:]]
                two[d] = two[d] + came
                total = jnp.concatenate(two, axis=2)
            else:
                total = terms[d] + rs_recv[p, d, step - 1].astype(F32)
            rs_send[p, d, step] = total.astype(BF16)
            later.append(send(rs_send.at[p, d, step], rs_recv.at[p, d, step], around[d]))
        return later

    def hidden_over_x(p):
        full = nt(down_in[...], cot[:, p].reshape(2 * PHASE, HALF)).astype(BF16)
        for half in range(2):
            some = full[:, half * PHASE : (half + 1) * PHASE]
            hg_send[p, :, half] = some.reshape(NX, SUB, PHASE)
        return [send(hg_send.at[p, xs[k]], hg_recv.at[p, k - 1], at(x_=xs[k])) for k in (2, 1, 3)]

    def hidden_sum(p, half):
        total = hg_send[p, x, half].astype(F32)
        for k in range(NX - 1):
            total = total + hg_recv[p, k, half].astype(F32)
        return total

    def hidden_pair(p, by_x):
        arrive(by_x)
        pair[p, 0] = hidden_sum(p, 1 - zl).astype(BF16)
        return send(pair.at[p, 0], pair.at[p, 1], partner)

    assemble(0)
    moving, by_x, by_pair = [None, None], [None, None], [None, None]
    for p in range(2):
        share(p, *tok_later[p])
        moving[p] = outset(p)
    assemble(1)
    assemble(2)
    moving[0] = onward(1, 0, moving[0])
    for m in (1, 3):
        cot_z[m].wait_recv()
        there = zhs[NZH - m]
        rows = cot.at[there // 2, there % 2, c]
        cot_core.append(send(rows, rows, at(c_=cs[1])))
    for k in (1, 3, 2):
        cot_y[k].wait_recv()
        rows = cot.at[far // 2, far % 2, c, ys[NY - k]]
        cot_core.append(send(rows, rows, at(c_=cs[1])))
    arrive(cot_core)
    by_x[0] = hidden_over_x(0)
    moving[1] = onward(1, 1, moving[1])
    by_x[1] = hidden_over_x(1)
    assemble(3)
    for p in range(2):
        moving[p] = onward(2, p, moving[p])
    by_pair[0] = hidden_pair(0, by_x[0])
    for p in range(2):
        moving[p] = onward(3, p, moving[p])
    by_pair[1] = hidden_pair(1, by_x[1])

    def chunk(there, p, step, d):
        if step == 3:
            return grads.at[there[1], p, :, there[0], :, halves[d]]
        return grads.at[there[1], p, :, there[0]]

    def forward(step, p):
        row = []
        for d in range(2):
            block = chunk(ring(-step if d == 0 else step), p, step, d)
            row.append(send(block, block, around[d]))
        return row

    for p in range(2):
        values = partial((zh, zl), p)
        hidden_grad = hidden_sum(p, zl)
        by_pair[p].wait_recv()
        hidden_grad = hidden_grad + pair[p, 1].astype(F32)
        for d in range(2):
            moving[p][d].wait_recv()
            values = values + rs_recv[p, d, 3].astype(F32)
        hidden, gate_grad, up_grad = local_step(values[0], values[1], hidden_grad)
        grads[zl, p, 0, zh] = gate_grad
        grads[zl, p, 1, zh] = up_grad
        moving[p] = forward(0, p)
        hid[zl, p, x] = hidden

    returned = {}

    def weight_grads(q):
        both = jnp.zeros((2 * SUB, HALF), F32)
        for half in range(2):
            for p in range(2):
                rows = grads[half, p, :, q].reshape(2 * SUB, PHASE)
                both = both + nn(rows, tok[half, p].reshape(PHASE, HALF))
        both = both.astype(BF16)
        for k in range(NX):
            here = both[:, k * 128 : (k + 1) * 128]
            wg_send[q, 0, k] = jnp.concatenate((here[:SUB, :64], here[SUB:, :64]), axis=1)
            wg_send[q, 1, k] = jnp.concatenate((here[:SUB, 64:], here[SUB:, 64:]), axis=1)
        wg_recv[q, c, x] = wg_send[q, c, x]
        return [
            send(wg_send.at[q, cs[e], xs[k]], wg_recv.at[q, c, x], at(x_=xs[k], c_=cs[e]))
            for k in (2, 1, 3, 0) for e in range(2) if (k, e) != (0, 0)
        ]

    def over_core(p):
        for half in range(2):
            term = tn(grads[half, p].reshape(8 * SUB, PHASE), gu[...].reshape(8 * SUB, HALF))
            part[p, half] = term.reshape(2, NY, 32, HALF)
        ta_send[p] = part[p, :, cs[1]].astype(BF16)
        return send(ta_send.at[p], ta_recv.at[p], at(c_=cs[1]))

    def over_y(p, by_core):
        by_core.wait_recv()
        total = part[p, :, c] + ta_recv[p].astype(F32)
        part[p, :, c] = total
        for k in range(NY):
            tb_send[p, k] = total[:, k].astype(BF16)
        return [send(tb_send.at[p, ys[k]], tb_recv.at[p, k - 1], at(y_=ys[k])) for k in (2, 1, 3)]

    def sum_y(p, by_y):
        arrive(by_y)
        total = part[p, :, c, y]
        for k in range(NY - 1):
            total = total + tb_recv[p, k].astype(F32)
        for k in range(NX):
            tc_send[:, p, k] = total[:, :, k * 128 : (k + 1) * 128].astype(BF16)

    turn = 2 * zl - 1
    finished = [zh, (zh + turn + NZH) % NZH, (zh - turn + NZH) % NZH, zhs[2]]
    for step in range(3):
        for p in range(2):
            arrive(moving[p])
            moving[p] = forward(step + 1, p)
        returned[step] = weight_grads(finished[step])
    by_pair = [send(hid.at[zl, p, x], hid.at[zl, p, x], partner) for p in range(2)]
    arrive(moving[0])
    by_core = over_core(0)
    for p in range(2):
        by_pair[p].wait_recv()
        own = hid.at[:, p, x]
        by_x[p] = {k: send(own, own, at(x_=xs[k])) for k in (1, 3)}
    early = over_y(0, by_core)
    arrive(moving[1])
    by_core = over_core(1)
    returned[3] = weight_grads(finished[3])
    late = over_y(1, by_core)
    for p in range(2):
        arrive(by_x[p].values())
        by_x[p] = []
        for half, k in ((0, 1), (1, 3)):
            passed = hid.at[half, p, xs[NX - k]]
            by_x[p].append(send(passed, passed, at(x_=xs[k])))
    sum_y(0, early)
    sum_y(1, late)
    by_place = [
        send(
            tc_send.at[zhs[m] // 2, zhs[m] % 2, xs[k]], tc_recv.at[zh, k], at(zh_=zhs[m], x_=xs[k])
        )
        for m in (2, 1, 3, 0) for k in (2, 1, 3, 0) if (m, k) != (0, 0)
    ]
    tc_recv[zh, 0] = tc_send[zh // 2, zh % 2, x]
    arrive(by_x[0])
    arrive(by_x[1])
    down = jnp.zeros((4 * SUB, HALF), F32)
    for half in range(2):
        for p in range(2):
            rows = hid[half, p].reshape(4 * SUB, PHASE)
            down = down + nn(rows, cot[half, p].reshape(PHASE, HALF))
    down_grad[...] = down
    stores = []

    def store(src, dst):
        stores.append(pltpu.make_async_copy(src, dst, load_sems.at[len(loads) + len(stores)]))
        stores[-1].start()

    store(down_grad, down_out)
    for step in range(4):
        arrive(returned[step])
        store(wg_recv.at[finished[step]], wg_out.at[finished[step]])
    arrive(by_place)
    for q in range(NZH):
        total = tc_recv[q, 0].astype(F32)
        for k in range(1, NX):
            total = total + tc_recv[q, k].astype(F32)
        token_grad[:, pl.ds(q * 128, 128)] = total
    store(token_grad, tg_out)
    for copy in started:
        copy.wait_send()
    for copy in stores:
        copy.wait()


def finish(tg_in, wg_in, down_in, tg_out, gate_out, up_out, down_out, tg, wg, down, gate, up, sems):
    loads = [pltpu.make_async_copy(wg_in.at[q], wg.at[q], sems.at[q]) for q in range(NZH)]
    loads.append(pltpu.make_async_copy(down_in, down, sems.at[NZH]))
    loads.append(pltpu.make_async_copy(tg_in, tg, sems.at[NZH + 1]))
    for load in loads:
        load.start()
    stores = []

    def store(src, dst):
        stores.append(pltpu.make_async_copy(src, dst, sems.at[len(loads) + len(stores)]))
        stores[-1].start()

    for q in range(NZH):
        loads[q].wait()
        here = pl.ds(q * 896, 896)
        block = wg[q].reshape(896, 128).T.astype(F32)
        for rows, buffer, out in ((block[:64], gate, gate_out), (block[64:], up, up_out)):
            buffer[:, here] = rows
            store(buffer.at[:, here], out.at[:, here])
        if q == 1:
            loads[NZH].wait()
            store(down, down_out)
            loads[NZH + 1].wait()
            store(tg, tg_out)
    for copy in stores:
        copy.wait()


def shards(tokens, cotangent, gate_weight, up_weight, down_weight):
    hbm = pl.BlockSpec(memory_space=pltpu.HBM)
    outs = [
        jax.ShapeDtypeStruct(tokens.shape, F32),
        jax.ShapeDtypeStruct(gate_weight.shape, F32),
        jax.ShapeDtypeStruct(up_weight.shape, F32),
        jax.ShapeDtypeStruct(down_weight.shape, F32),
    ]
    between = [
        outs[0],
        jax.ShapeDtypeStruct((NZH, 2, NX, SUB, 128), BF16),
        outs[3],
    ]
    scratch = [
        pltpu.VMEM(tokens.shape, BF16),
        pltpu.VMEM(cotangent.shape, BF16),
        pltpu.VMEM(gate_weight.shape, BF16),
        pltpu.VMEM(up_weight.shape, BF16),
        pltpu.VMEM(down_weight.shape, BF16),
        pltpu.VMEM((NZH, 2, NX, SUB, 128), BF16),
        pltpu.VMEM((2 * NX, NZH, SUB, 128), BF16),
        pltpu.VMEM((2, NZH, SUB, HALF), BF16),
        pltpu.VMEM((2, 2, 2, NY, 32, HALF), BF16),
        pltpu.VMEM((2, 2, 2, NY, 32, HALF), BF16),
        pltpu.VMEM((2, 2, 4, 2, SUB, PHASE), BF16),
        pltpu.VMEM((2, 2, 4, 2, SUB, PHASE), BF16),
        pltpu.VMEM((2, NX, 2, SUB, PHASE), BF16),
        pltpu.VMEM((2, NX - 1, 2, SUB, PHASE), BF16),
        pltpu.VMEM((2, 2, SUB, PHASE), BF16),
        pltpu.VMEM((2, 2, 2, NZH, SUB, PHASE), BF16),
        pltpu.VMEM((2, 2, NX, SUB, PHASE), BF16),
        pltpu.VMEM((NZH, 2, NX, SUB, 128), BF16),
        pltpu.VMEM((NZH, 2, NX, SUB, 128), BF16),
        pltpu.VMEM((2, 2, 2, NY, 32, HALF), F32),
        pltpu.VMEM((2, 2, NY, 32, HALF), BF16),
        pltpu.VMEM((2, 2, NY, 32, HALF), BF16),
        pltpu.VMEM((2, NY, 2, 32, HALF), BF16),
        pltpu.VMEM((2, NY - 1, 2, 32, HALF), BF16),
        pltpu.VMEM((2, 2, NX, 32, 128), BF16),
        pltpu.VMEM((NZH, NX, 32, 128), BF16),
        pltpu.VMEM(down_weight.shape, F32),
        pltpu.VMEM(tokens.shape, F32),
        pltpu.SemaphoreType.DMA((11,)),
        pltpu.SemaphoreType.DMA((COPIES,)),
        pltpu.SemaphoreType.DMA((COPIES,)),
    ]
    token_grad, weight_grad, down_grad = pl.pallas_call(
        kernel,
        out_shape=between,
        in_specs=[hbm] * 5,
        out_specs=[hbm] * 3,
        scratch_shapes=scratch,
        compiler_params=pltpu.CompilerParams(
            collective_id=0, has_side_effects=True, vmem_limit_bytes=60 * 2**20
        ),
        name="layer",
    )(tokens, cotangent, gate_weight, up_weight, down_weight)
    return pl.pallas_call(
        finish,
        out_shape=outs,
        in_specs=[hbm] * 3,
        out_specs=[hbm] * 4,
        scratch_shapes=[
            pltpu.VMEM(tokens.shape, F32),
            pltpu.VMEM((NZH, 2, NX, SUB, 128), BF16),
            pltpu.VMEM(down_weight.shape, F32),
            pltpu.VMEM(gate_weight.shape, F32),
            pltpu.VMEM(up_weight.shape, F32),
            pltpu.SemaphoreType.DMA((NZH + 2 + 2 * NZH + 2,)),
        ],
        compiler_params=pltpu.CompilerParams(vmem_limit_bytes=60 * 2**20),
        name="finish",
    )(token_grad, weight_grad, down_grad)


def solution(mesh):
    return jax.shard_map(
        shards,
        mesh=mesh,
        in_specs=(
            P(("dep", "out"), "inp"),
            P(("dep", "out"), "inp"),
            P(("inp", "dep"), "out"),
            P(("inp", "dep"), "out"),
            P(("out", "dep"), "inp"),
        ),
        out_specs=(
            P(("dep", "out"), "inp"),
            P(("inp", "dep"), "out"),
            P(("inp", "dep"), "out"),
            P(("out", "dep"), "inp"),
        ),
        check_vma=False,
    )
```
